32 devices in a mesh: mem: 4 (over z), lat: 4 (over y, x), lon: 2 (over core).
Axes of the slice: x: 2, y: 2, z: 4, core: 2. Of those that a mesh axis runs over, the one named last changes fastest.
Arguments:
- perturbation: bfloat16 [16, 64, 128, 256], P('mem', None, 'lat', 'lon'), may hold values from -6 to 6
- control: bfloat16 [16, 16, 128, 256], P('mem', None, 'lat', 'lon'), may hold values from -6 to 6
- filter_length: float32 [16], replicated, may hold values from 20 to 2000
- modes: float32 [64, 16], replicated, may hold values from -1.5 to 1.5
- obs_weights: bfloat16 [4096, 64], P(('lat', 'lon')), may hold values from -1.5 to 1.5
- innovation: float32 [4096], P(('lat', 'lon')), may hold values from -6 to 6
- obs_tile: int32 [4096, 1], P(('lat', 'lon')), may hold values from 0 to 7; in each aligned block of 512 rows (0 to 511, 512 to 1023, ...) at most 128 rows name the same one
- obs_column: int32 [4096], P(('lat', 'lon')), may hold values from 0 to 16383
- obs_count: int32 [8], P(('lat', 'lon')), may hold values from 64 to 512, as said below
Outputs:
- increment: float32 [64, 128, 256], P('mem', 'lat', 'lon')
- departures: float32 [4096], P(('lat', 'lon'))
The draws below stay inside these ranges and needn't reach their ends.
Inputs may be any that keep to these rules, and one draw needn't show every extreme that they name: obs_tile names each tile for at most 128 of the 512 slots of one tile, a bound that some block reaches of them. `obs_count`: some tile has all 512 slots live.
All inputs are finite; a program needn't handle non-finite values.
Results may differ from the reference program's by a relative error of at most 0.0003.
Values sent between devices are 32-bit elements; how exact they have to be, the bound alone decides.
No kernel may reach another device: no remote copies, remote signals or barrier semaphores. Data moves between devices by JAX's collectives and lax.ppermute only.
A program may use at most 64 MiB of HBM per device.

```python
import math
import jax
import jax.numpy as jnp
import numpy as np
from jax import lax

CX = 32
CY = 128
LEV = 64
MODES = 16
OBS_DEV = 512
TILES = 8
CAP = 128
MEMBERS = 16
NX = 128
NY = 256
OBS = 4096
N_LAT = 4
N_LON = 2


def draw_obs_count(key, part):
    first, second = jax.random.split(jax.random.fold_in(key, 11))
    counts = jax.random.randint(first, (TILES,), OBS_DEV // 8, OBS_DEV + 1)
    chosen = jax.random.randint(second, (), 0, TILES)
    return counts.at[chosen].set(OBS_DEV).astype(jnp.int32)


def place_ends(values, rng, least, high):
    longest = values.shape.index(max(values.shape))
    spots = []
    for shift in (0, 1):
        where = [jax.random.randint(jax.random.fold_in(rng, axis), (), 0, length) for axis, length in enumerate(values.shape)]
        where[longest] = (where[longest] + shift) % values.shape[longest]
        spots.append(tuple(where))
    return values.at[spots[0]].set(least).at[spots[1]].set(high)


def block_scale(own_key, dims, shards, low, largest):
    def one(axis_at, shards_of):
        heights = jax.random.uniform(jax.random.fold_in(jax.random.fold_in(own_key, 6), axis_at), (shards_of,), jnp.float32, low / len(shards), largest / len(shards))
        return jnp.repeat(jnp.exp(heights), dims[axis_at] // shards_of).reshape((-1,) + (1,) * (len(dims) - axis_at - 1))

    factor_of = one(*shards[0])
    for cut in shards[1:]:
        factor_of = factor_of * one(*cut)
    return factor_of


def deal_out(own_key, own, number, rows, amount, top, reach, skew):
    order = jax.random.permutation(own_key, amount)
    crowded, ordinary = load_shares(amount, rows * top, reach, skew, True), load_shares(amount, rows * top, reach, skew, False)
    places = jnp.arange(amount)

    def named(sizes, offset_by):
        used = int((sizes > 0).sum())
        fixed = max(1, used // 4)
        passed = fixed + (places - fixed + offset_by * (used - fixed)) % max(1, amount - fixed)
        return jnp.zeros((amount,), jnp.int32).at[order[jnp.where(places < fixed, places, passed)]].set(jnp.asarray(sizes, jnp.int32))

    sizes = jnp.where(number % 4 == 0, named(crowded, number // 4), named(ordinary, number - number // 4 - 1))
    mixed = jax.random.permutation(jax.random.fold_in(own, 3), amount)
    giver, taker = mixed[0:amount // 2 * 2:2], mixed[1:amount // 2 * 2:2]
    margin = jnp.minimum(sizes[giver] - 1, reach - sizes[taker]) // 2
    margin = jnp.where((giver == order[0]) | (taker == order[0]) | (sizes[taker] == 0), 0, jnp.maximum(margin, 0))
    passed = jax.random.randint(jax.random.fold_in(own, 4), (amount // 2,), 0, 1 << 20) % (margin + 1)
    sizes = sizes.at[giver].add(-passed).at[taker].add(passed)
    labels = jnp.searchsorted(jnp.cumsum(sizes), jnp.arange(rows * top), side="right").astype(jnp.int32)
    listing = labels.reshape(top, rows).T
    listing = listing[jax.random.permutation(jax.random.fold_in(own, 1), rows)]
    offset_by = jax.random.randint(jax.random.fold_in(own, 2), (rows, 1), 0, top)
    return jnp.take_along_axis(listing, (jnp.arange(top)[None, :] + offset_by) % top, axis=1)


def load_shares(number_of, total, reach, lean, full):
    portions = [(1 << 20) // math.isqrt(rank ** lean) + 1 for rank in range(1, number_of + 1)]
    largest = reach if full else min(reach, max(-(-total // number_of), total * portions[0] // sum(portions)))
    least = 1 if total - largest >= number_of - 1 else 0
    holding, spare = [largest] + [least] * (number_of - 1), total - largest - least * (number_of - 1)
    while spare > 0:
        movable = [i for i in range(1, number_of) if holding[i] < largest] or [i for i in range(1, number_of) if holding[i] < reach]
        whole, left = sum([portions[i] for i in movable]), spare
        for i in movable:
            more = min(reach - holding[i], max(1, left * portions[i] // whole), spare)
            holding[i] = holding[i] + more
            spare = spare - more
    return np.array(holding)


def normal_values(stream_key, dims, width, limit, cuts=(), kind=jnp.bfloat16):
    array = jax.random.normal(stream_key, dims, jnp.float32) * width
    if len(cuts) > 0:
        array = block_scale(stream_key, dims, cuts, -0.22, 0.18) * array
    return jnp.clip(array, min=-limit, max=limit).astype(kind)


def setup_inputs(seed: int = 0) -> dict:
    keys = jax.random.split(jax.random.key(seed), 10)
    perturbation = normal_values(keys[0], (MEMBERS, LEV, NX, NY), 1.0, 6.0, ((0, 4), (2, 4), (3, 2)))
    control = normal_values(keys[1], (MEMBERS, MODES, NX, NY), 1.0, 6.0, ((0, 4), (2, 4), (3, 2)))
    filter_length = jnp.clip(jnp.exp(jax.random.uniform(keys[2], (MODES,), jnp.float32, math.log(20.0), math.log(2000.0))), 20.0, 2000.0)
    modes = normal_values(keys[3], (LEV, MODES), MODES ** -0.5, 1.5, (), jnp.float32)
    obs_weights = normal_values(keys[4], (OBS, LEV), 0.25, 1.5, ((0, 8),))
    innovation = normal_values(keys[5], (OBS,), 1.0, 6.0, ((0, 8),), jnp.float32)
    obs_tile_keys = jax.random.split(jax.random.fold_in(keys[6], 1), OBS // OBS_DEV)
    obs_tile_turns = jax.random.permutation(jax.random.fold_in(keys[6], 3), OBS // OBS_DEV)
    obs_tile = jax.vmap(lambda own, number: deal_out(jax.random.fold_in(keys[6], 2), own, number, OBS_DEV, TILES, 1, CAP, 2))(obs_tile_keys, obs_tile_turns).reshape((OBS, 1))
    obs_column = place_ends(jax.random.randint(keys[7], (OBS,), 0, 4 * CX * CY), jax.random.fold_in(keys[7], 1), 0, (4 * CX * CY) - 1).astype(jnp.int32)
    obs_count = draw_obs_count(jax.random.fold_in(keys[9], 71), 0)
    return {"perturbation": perturbation, "control": control, "filter_length": filter_length, "modes": modes, "obs_weights": obs_weights, "innovation": innovation, "obs_tile": obs_tile, "obs_column": obs_column, "obs_count": obs_count}


def sweep(field, rate, axis, backward):
    moved = jnp.moveaxis(field, axis, 0)
    decay = rate[:, None]

    def advance(carry, row):
        fresh = decay * carry + (1.0 - decay) * row
        return (fresh, fresh)
    _, result = lax.scan(advance, jnp.zeros_like(moved[0]), moved, reverse=backward)
    return jnp.moveaxis(result, 0, axis)

def reference(perturbation, control, filter_length, modes, obs_weights, innovation, obs_tile, obs_column, obs_count):
    rate = jnp.exp(-1.0 / filter_length)
    boost = (1.0 + rate) / (1.0 - rate)
    members = perturbation.shape[0]

    def member_step(total, pieces):
        member_pert, member_control = pieces
        field = member_control.astype(jnp.float32) * boost[:, None, None]
        field = sweep(field, rate, 1, False)
        field = sweep(field, rate, 1, True)
        field = sweep(field, rate, 2, False)
        field = sweep(field, rate, 2, True)
        profile = jnp.einsum('zk,kxy->zxy', modes, field, precision=lax.Precision.HIGHEST)
        return (total + member_pert.astype(jnp.float32) * profile, None)
    start = jnp.zeros(perturbation.shape[1:], jnp.float32)
    summed, _ = lax.scan(member_step, start, (perturbation, control))
    increment = summed * (1.0 / math.sqrt(members - 1))
    tile_rows = NX // N_LAT
    tile_cols = NY // N_LON
    target = obs_tile[:, 0]
    fine_row = target // N_LON * 2 * tile_rows + obs_column // (2 * tile_cols)
    fine_col = target % N_LON * 2 * tile_cols + obs_column % (2 * tile_cols)
    padded = jnp.pad(increment, ((0, 0), (1, 1), (1, 1)))
    near_row = fine_row // 2 + 1
    far_row = near_row + 2 * (fine_row % 2) - 1
    near_col = fine_col // 2 + 1
    far_col = near_col + 2 * (fine_col % 2) - 1
    blend = 0.5625 * padded[:, near_row, near_col] + 0.1875 * padded[:, far_row, near_col] + 0.1875 * padded[:, near_row, far_col] + 0.0625 * padded[:, far_row, far_col]
    equivalent = lax.optimization_barrier(jnp.sum(obs_weights.astype(jnp.float32).T * blend, axis=0))
    places = jnp.arange(innovation.shape[0], dtype=jnp.int32)
    valid = places % OBS_DEV < obs_count[places // OBS_DEV]
    departures = jnp.where(valid, innovation - equivalent, 0.0)
    return (increment, departures)
```

```python
import functools
import math

import jax
import jax.numpy as jnp
from jax import lax
from jax.experimental import pallas as pl
from jax.experimental.pallas import tpu as pltpu
from jax.sharding import PartitionSpec as P

F32, BF16 = jnp.float32, jnp.bfloat16
VMEM = pl.BlockSpec(memory_space=pltpu.VMEM)
SMEM = pl.BlockSpec(memory_space=pltpu.SMEM)


def params(flops, moved):
    return dict(
        compiler_params=pltpu.CompilerParams(vmem_limit_bytes=48 * 2**20),
        cost_estimate=pl.CostEstimate(flops=flops, bytes_accessed=moved, transcendentals=0),
    )


def paired(count):
    return count & (count - 1) == 0


def toward(place, step, count):
    return place ^ step if paired(count) else (place + step) % count


def source(place, step, count):
    return place ^ step if paired(count) else (place - step) % count


def send(block, axis, step):
    count = lax.axis_size(axis)
    return lax.ppermute(block, axis, [(i, toward(i, step, count)) for i in range(count)])


def collect(block, axis):
    count = lax.axis_size(axis)
    blocks = block[None]
    if not paired(count):
        return jnp.concatenate([blocks] + [send(blocks, axis, s) for s in range(1, count)])
    step = 1
    while step < count:
        blocks = jnp.concatenate([blocks, send(blocks, axis, step)])
        step *= 2
    return blocks


def halve(value):
    high = value.astype(BF16)
    return high, (value - high.astype(F32)).astype(BF16)


def columns_kernel(own_ref, other_ref, matrix_ref, decay_ref, field_ref, edge_ref, first):
    members, modes, rows, cols = own_ref.shape
    sources = matrix_ref.shape[0]
    lines = members * modes
    for k in range(modes):
        pieces = [jnp.concatenate([own_ref[m, k] for m in range(members)])]
        for s in range(1, sources):
            pieces.append(
                jnp.concatenate([other_ref[s - 1, m, k] for m in range(members)]).astype(BF16)
            )
        split = [halve(matrix_ref[s, k]) for s in range(sources)]
        weights = jnp.concatenate(
            [jnp.concatenate([high, low], axis=1) for high, low in split], axis=0
        )
        both = jnp.dot(jnp.concatenate(pieces, axis=1), weights, preferred_element_type=F32)
        made = both[:, :cols] + both[:, cols:]
        for m in range(members):
            field_ref[pl.ds(m * modes + k, rows, stride=lines), :] = made[m * rows : (m + 1) * rows]
    decay = decay_ref[...]
    state = jnp.zeros((lines, cols), F32)
    for x in range(rows):
        state = decay * state + field_ref[x * lines : (x + 1) * lines, :]
        first[x * lines : (x + 1) * lines, :] = state
    edge_ref[0] = state
    state = jnp.zeros((lines, cols), F32)
    for x in reversed(range(rows)):
        state = decay * state + first[x * lines : (x + 1) * lines, :]
    edge_ref[1] = state


def sum_kernel(
    places_ref, chunks_ref, table_ref, edges_ref, field_ref, modes_ref, pert_ref, *rest
):
    chunks = len(rest) - 3
    outs, (first, second, pert) = rest[:chunks], rest[chunks:]
    members, levels, rows, cols = pert_ref.shape
    lines = table_ref.shape[1]
    share = levels // chunks
    count = edges_ref.shape[0]

    for m in range(members):
        for z in range(levels):
            at = (m * levels + z) * rows
            pert[at : at + rows, :] = pert_ref[m, z].astype(F32)

    log, decay, beta = table_ref[0], table_ref[1], table_ref[2]

    def power(ahead):
        exponent = (rows * jnp.maximum(ahead, 0)).astype(F32)
        return jnp.where(ahead >= 0, jnp.exp(log * exponent), 0.0)

    own = places_ref[0]
    state = jnp.zeros((lines, cols), F32)
    after = jnp.zeros((lines, cols), F32)
    for s in range(count):
        there = places_ref[s]
        state = state + power(own - there - 1) * edges_ref[s, 0]
        before = jnp.zeros((lines, cols), F32)
        for t in range(count):
            before = before + power(there - places_ref[t] - 1) * edges_ref[t, 0]
        after = after + power(there - own - 1) * (edges_ref[s, 1] + beta * before)

    for x in range(rows):
        state = decay * state + field_ref[x * lines : (x + 1) * lines, :]
        first[x * lines : (x + 1) * lines, :] = state
    state = after
    for x in reversed(range(rows)):
        state = decay * state + first[x * lines : (x + 1) * lines, :]
        high, low = halve(state)
        second[:, x * cols : (x + 1) * cols] = jnp.concatenate([high, low, high])

    for pair in range(0, rows, 2):
        profile = jnp.dot(
            modes_ref[...],
            second[:, pair * cols : (pair + 2) * cols],
            preferred_element_type=F32,
        )
        for half in range(2):
            x = pair + half
            for r in range(chunks):
                total = None
                for m in range(members):
                    at = (m * levels + chunks_ref[r] * share) * rows + x
                    line = m * levels + r * share
                    term = (
                        profile[line : line + share, half * cols : (half + 1) * cols]
                        * pert[pl.ds(at, share, stride=rows), :]
                    )
                    total = term if total is None else total + term
                outs[r][pl.ds(x, share, stride=rows), :] = total


def observe_kernel(levels, rows, chunks_ref, spots_ref, origin_ref, packed_ref, *rest):
    chunks = len(rest) - 2
    sums, out_ref, split = rest[:chunks], rest[chunks], rest[chunks + 1]
    blocks, _, slots = packed_ref.shape
    step, cols = sums[0].shape
    for r in range(chunks):
        high, low = halve(sums[r][...])
        at = pl.multiple_of(chunks_ref[r] * step, step)
        split[pl.ds(at, step), :] = jnp.concatenate([high, low], axis=1)

    def spread(fine, origin, length):
        near = jnp.floor(fine * 0.5)
        far = near - 1.0 + 2.0 * (fine - 2.0 * near)
        cell = (lax.broadcasted_iota(jnp.int32, (length, slots), 0) + origin).astype(F32)
        return jnp.where(cell == near, 0.75, 0.0) + jnp.where(cell == far, 0.25, 0.0)

    group = math.gcd(levels, 16)

    @pl.loop(0, blocks)
    def _(block):
        fine = packed_ref[block, levels : levels + 8, :]
        across = spread(fine[1:2], origin_ref[1], cols).astype(BF16)
        across = jnp.concatenate([across, across])
        down = spread(fine[0:1], origin_ref[0], rows)
        total = jnp.zeros((rows, slots), F32)
        for g in range(0, levels, group):
            seen = jnp.dot(
                split[g * rows : (g + group) * rows, :], across, preferred_element_type=F32
            )
            weights = packed_ref[block, g : g + group, :]
            for z in range(group):
                total = total + seen[z * rows : (z + 1) * rows] * weights[z : z + 1]
        out_ref[pl.ds(spots_ref[block], 1), :] = jnp.sum(total * down, axis=0, keepdims=True)


def per_device(
    perturbation,
    control,
    filter_length,
    modes,
    obs_weights,
    innovation,
    obs_tile,
    obs_column,
    obs_count,
):
    members, levels, rows, cols = perturbation.shape
    kinds = control.shape[1]
    lines = members * kinds
    n_mem, n_lat, n_lon = (lax.axis_size(a) for a in ("mem", "lat", "lon"))
    mem, lat, lon = (lax.axis_index(a) for a in ("mem", "lat", "lon"))
    slots = innovation.shape[0]
    share = levels // n_mem
    all_cols = cols * n_lon

    rate = jnp.exp(-1.0 / filter_length)
    rest = 1.0 - rate
    log = jnp.log1p(-rest)
    beta = rate * jnp.expm1(2.0 * rows * log) / jnp.expm1(2.0 * log)
    table = jnp.broadcast_to(
        jnp.tile(jnp.stack([log, rate, beta]), (1, members))[:, :, None], (3, lines, cols)
    )
    to_col = (lon * cols + jnp.arange(cols))[None, None, None, :]
    lons = jnp.stack([source(lon, s, n_lon) for s in range(n_lon)])
    from_col = (lons[:, None] * cols + jnp.arange(cols)[None, :])[:, None, :, None]
    log4 = log[None, :, None, None]
    reach = (all_cols - jnp.maximum(to_col, from_col)).astype(F32)
    matrix = (
        (rest * rest)[None, :, None, None]
        * jnp.exp(jnp.abs(to_col - from_col).astype(F32) * log4)
        * -jnp.expm1(2.0 * reach * log4)
    )

    valid = jnp.arange(slots, dtype=jnp.int32) < obs_count[0]
    target = obs_tile[:, 0]
    fine_row = target // n_lon * (2 * rows) + obs_column // (2 * cols)
    fine_col = target % n_lon * (2 * cols) + obs_column % (2 * cols)
    weights = jnp.where(valid[:, None], obs_weights.astype(F32), 0.0).T
    places = jnp.stack([fine_row, fine_col]).astype(F32)
    packed = jnp.concatenate([weights, places, jnp.zeros((6, slots), F32)])

    whole = control.astype(F32)
    others = [send(whole, "lon", s) for s in range(1, n_lon)]
    others = jnp.stack(others) if others else jnp.zeros((1,) + whole.shape, F32)
    field, edge = pl.pallas_call(
        columns_kernel,
        out_shape=(
            jax.ShapeDtypeStruct((rows * lines, cols), F32),
            jax.ShapeDtypeStruct((2, lines, cols), F32),
        ),
        in_specs=[VMEM] * 4,
        out_specs=(VMEM, VMEM),
        scratch_shapes=[pltpu.VMEM((rows * lines, cols), F32)],
        **params(2 * 2 * lines * rows * cols * all_cols, 4 * 2**20),
    )(control, others, matrix, table[1])

    edges = collect(edge, "lat")
    packed = collect(packed, "lat")
    packed = collect(packed, "lon").reshape((n_lat * n_lon,) + packed.shape[1:])
    lats = jnp.stack([source(lat, s, n_lat) for s in range(n_lat)]).astype(jnp.int32)
    chunks = jnp.stack([toward(mem, r, n_mem) for r in range(n_mem)]).astype(jnp.int32)
    scaled = modes * (1.0 / math.sqrt(members * n_mem - 1))
    scaled = jnp.concatenate(
        [lax.dynamic_slice_in_dim(scaled, toward(mem, r, n_mem) * share, share) for r in range(n_mem)]
    )
    spread = (
        jnp.eye(members, dtype=F32)[:, None, :, None] * scaled[None, :, None, :]
    ).reshape(members * levels, lines)
    high = lax.reduce_precision(spread, 8, 7)
    spread = jnp.concatenate([high, high, spread - high], axis=1).astype(BF16)
    chunk_shape = jax.ShapeDtypeStruct((share * rows, cols), F32)
    sums = pl.pallas_call(
        sum_kernel,
        out_shape=(chunk_shape,) * n_mem,
        in_specs=[SMEM, SMEM] + [VMEM] * 5,
        out_specs=(VMEM,) * n_mem,
        scratch_shapes=[
            pltpu.VMEM((rows * lines, cols), F32),
            pltpu.VMEM((3 * lines, rows * cols), BF16),
            pltpu.VMEM((members * levels * rows, cols), F32),
        ],
        **params(6 * members * levels * lines * rows * cols, 6 * 2**20),
    )(lats, chunks, table, edges, field, spread, perturbation)

    held = list(sums)
    if paired(n_mem):
        step = 1
        while step < n_mem:
            for r in reversed(range(step, n_mem, 2 * step)):
                held[r ^ step] = held[r ^ step] + send(held[r], "mem", step)
            step *= 2
    else:
        for r in range(1, n_mem):
            held[0] = held[0] + send(held[r], "mem", r)
    increment = held[0].reshape(share, rows, cols)

    lons = lons.astype(jnp.int32)
    spots = (lats[None, :] * n_lon + lons[:, None]).reshape(-1)
    origin = jnp.stack([lat * rows, lon * cols]).astype(jnp.int32)
    partial = pl.pallas_call(
        functools.partial(observe_kernel, levels, rows),
        out_shape=jax.ShapeDtypeStruct((n_lat * n_lon, slots), F32),
        in_specs=[SMEM] * 3 + [VMEM] * (1 + n_mem),
        out_specs=VMEM,
        scratch_shapes=[pltpu.VMEM((levels * rows, 2 * cols), BF16)],
        **params(4 * levels * rows * cols * n_lat * n_lon * slots, 4 * 2**20),
    )(chunks, spots, origin, packed, *sums)
    spread_out = jnp.broadcast_to(partial[None], (n_mem,) + partial.shape)
    spread_out = spread_out.reshape(n_mem * n_lat * n_lon, slots)
    back = lax.all_to_all(spread_out, ("mem", "lat", "lon"), 0, 0, tiled=True)
    departures = jnp.where(valid, innovation - jnp.sum(back, axis=0), 0.0)
    return (increment, departures)


def solution(mesh):
    placed = (
        P("mem", None, "lat", "lon"),
        P("mem", None, "lat", "lon"),
        P(),
        P(),
        P(("lat", "lon"), None),
        P(("lat", "lon")),
        P(("lat", "lon"), None),
        P(("lat", "lon")),
        P(("lat", "lon")),
    )
    return jax.shard_map(
        per_device,
        mesh=mesh,
        in_specs=placed,
        out_specs=(P("mem", "lat", "lon"), P(("lat", "lon"))),
        check_vma=False,
    )
```

```python
import functools
import math

import jax
import jax.numpy as jnp
from jax import lax
from jax.experimental import pallas as pl
from jax.experimental.pallas import tpu as pltpu
from jax.sharding import PartitionSpec as P

F32, BF16 = jnp.float32, jnp.bfloat16
VMEM = pl.BlockSpec(memory_space=pltpu.VMEM)
SMEM = pl.BlockSpec(memory_space=pltpu.SMEM)


def params(flops, moved, held):
    return dict(
        compiler_params=pltpu.CompilerParams(vmem_limit_bytes=held + 6 * 2**20),
        cost_estimate=pl.CostEstimate(flops=flops, bytes_accessed=moved, transcendentals=0),
    )


def paired(count):
    return count & (count - 1) == 0


def toward(place, step, count):
    return place ^ step if paired(count) else (place + step) % count


def source(place, step, count):
    return place ^ step if paired(count) else (place - step) % count


def send(block, axis, step):
    count = lax.axis_size(axis)
    return lax.ppermute(block, axis, [(i, toward(i, step, count)) for i in range(count)])


def collect(block, axis):
    count = lax.axis_size(axis)
    blocks = block[None]
    if not paired(count):
        return jnp.concatenate([blocks] + [send(blocks, axis, s) for s in range(1, count)])
    step = 1
    while step < count:
        blocks = jnp.concatenate([blocks, send(blocks, axis, step)])
        step *= 2
    return blocks


def halve(value):
    high = value.astype(BF16)
    return high, (value - high.astype(F32)).astype(BF16)


def matrix_kernel(starts_ref, log_ref, to_ref, from_ref, matrix_ref):
    sources, cols, modes = from_ref.shape
    across = lax.broadcasted_iota(jnp.int32, (cols, cols), 1) + starts_ref[0]
    for s in range(sources):
        down = lax.broadcasted_iota(jnp.int32, (cols, cols), 0) + starts_ref[s]
        distance = jnp.abs(across - down).astype(F32)
        for k in range(modes):
            end = jnp.where(across >= down, to_ref[k : k + 1, :], from_ref[s, :, k : k + 1])
            high, low = halve(jnp.exp(distance * log_ref[k]) * end)
            at = s * cols
            matrix_ref[k, at : at + cols, :] = jnp.concatenate([high, low], axis=1)


def columns_kernel(own_ref, other_ref, matrix_ref, table_ref, field_ref, edge_ref, first):
    members, modes, rows, cols = own_ref.shape
    sources = matrix_ref.shape[1] // cols
    lines = members * modes
    for k in range(modes):
        pieces = [jnp.concatenate([own_ref[m, k] for m in range(members)])]
        for s in range(1, sources):
            pieces.append(
                jnp.concatenate([other_ref[s - 1, m, k] for m in range(members)]).astype(BF16)
            )
        both = jnp.dot(
            jnp.concatenate(pieces, axis=1), matrix_ref[k], preferred_element_type=F32
        )
        made = both[:, :cols] + both[:, cols:]
        for m in range(members):
            field_ref[pl.ds(m * modes + k, rows, stride=lines), :] = made[m * rows : (m + 1) * rows]
    decay = jnp.broadcast_to(table_ref[:, 1:2], (lines, cols))
    state = jnp.zeros((lines, cols), F32)
    for x in range(rows):
        state = decay * state + field_ref[x * lines : (x + 1) * lines, :]
        first[x * lines : (x + 1) * lines, :] = state
    edge_ref[0] = state
    state = jnp.zeros((lines, cols), F32)
    for x in reversed(range(rows)):
        state = decay * state + first[x * lines : (x + 1) * lines, :]
    edge_ref[1] = state


def sum_kernel(
    scale, places_ref, chunks_ref, table_ref, edges_ref, field_ref, modes_ref, pert_ref, *rest
):
    chunks = len(rest) - 3
    outs, (first, second, pert) = rest[:chunks], rest[chunks:]
    members, levels, rows, cols = pert_ref.shape
    lines, kinds = table_ref.shape[0], table_ref.shape[0] // members
    share = levels // chunks
    count = edges_ref.shape[0]

    for m in range(members):
        for z in range(levels):
            at = (m * levels + z) * rows
            pert[at : at + rows, :] = pert_ref[m, z].astype(F32)

    log, decay, beta = (
        jnp.broadcast_to(table_ref[:, i : i + 1], (lines, cols)) for i in range(3)
    )

    def power(ahead):
        exponent = (rows * jnp.maximum(ahead, 0)).astype(F32)
        return jnp.where(ahead >= 0, jnp.exp(log * exponent), 0.0)

    own = places_ref[0]
    state = jnp.zeros((lines, cols), F32)
    after = jnp.zeros((lines, cols), F32)
    for s in range(count):
        there = places_ref[s]
        state = state + power(own - there - 1) * edges_ref[s, 0]
        before = jnp.zeros((lines, cols), F32)
        for t in range(count):
            before = before + power(there - places_ref[t] - 1) * edges_ref[t, 0]
        after = after + power(there - own - 1) * (edges_ref[s, 1] + beta * before)

    for x in range(rows):
        state = decay * state + field_ref[x * lines : (x + 1) * lines, :]
        first[x * lines : (x + 1) * lines, :] = state
    state = after
    for x in reversed(range(rows)):
        state = decay * state + first[x * lines : (x + 1) * lines, :]
        high, low = halve(state)
        second[:, x * cols : (x + 1) * cols] = jnp.concatenate([high, low, high])

    held = jnp.concatenate([modes_ref[pl.ds(chunks_ref[r] * share, share), :] for r in range(chunks)])
    held = jnp.concatenate([held * scale] * members, axis=1)
    member = lax.broadcasted_iota(jnp.int32, (levels, lines), 1) // kinds
    high, low = halve(
        jnp.concatenate([jnp.where(member == m, held, 0.0) for m in range(members)])
    )
    weights = jnp.concatenate([high, high, low], axis=1)

    for pair in range(0, rows, 2):
        profile = jnp.dot(
            weights,
            second[:, pair * cols : (pair + 2) * cols],
            preferred_element_type=F32,
        )
        for half in range(2):
            x = pair + half
            for r in range(chunks):
                total = None
                for m in range(members):
                    at = (m * levels + chunks_ref[r] * share) * rows + x
                    line = m * levels + r * share
                    term = (
                        profile[line : line + share, half * cols : (half + 1) * cols]
                        * pert[pl.ds(at, share, stride=rows), :]
                    )
                    total = term if total is None else total + term
                outs[r][pl.ds(x, share, stride=rows), :] = total


def observe_kernel(levels, rows, chunks_ref, origin_ref, spots_ref, *rest):
    chunks, tiles = chunks_ref.shape[0], spots_ref.shape[0]
    sums, packs, (out_ref, split) = rest[:chunks], rest[chunks:-2], rest[-2:]
    slots = out_ref.shape[1]
    step, cols = sums[0].shape
    for r in range(chunks):
        high, low = halve(sums[r][...])
        at = pl.multiple_of(chunks_ref[r] * step, step)
        split[pl.ds(at, step), :] = jnp.concatenate([high, low], axis=1)

    def spread(fine, origin, length):
        near = jnp.floor(fine * 0.5)
        far = near - 1.0 + 2.0 * (fine - 2.0 * near)
        cell = (lax.broadcasted_iota(jnp.int32, (length, slots), 0) + origin).astype(F32)
        return jnp.where(cell == near, 0.75, 0.0) + jnp.where(cell == far, 0.25, 0.0)

    group = math.gcd(levels, 16)
    before = 0
    for packed_ref in packs:

        @pl.loop(0, packed_ref.shape[0])
        def _(block, packed_ref=packed_ref, before=before):
            fine = packed_ref[block, levels : levels + 8, :]
            across = spread(fine[1:2], origin_ref[1], cols).astype(BF16)
            across = jnp.concatenate([across, across])
            down = spread(fine[0:1], origin_ref[0], rows)
            total = jnp.zeros((rows, slots), F32)
            for g in range(0, levels, group):
                seen = jnp.dot(
                    split[g * rows : (g + group) * rows, :], across, preferred_element_type=F32
                )
                weights = packed_ref[block, g : g + group, :]
                for z in range(group):
                    total = total + seen[z * rows : (z + 1) * rows] * weights[z : z + 1]
            row = jnp.sum(total * down, axis=0, keepdims=True)
            for copy in range(out_ref.shape[0] // tiles):
                out_ref[pl.ds(copy * tiles + spots_ref[before + block], 1), :] = row

        before += packed_ref.shape[0]


def finish_kernel(count_ref, innovation_ref, back_ref, *rest):
    parts, (increment_ref, departures_ref) = rest[:-2], rest[-2:]
    total = parts[0][...]
    for part in parts[1:]:
        total = total + part[...]
    increment_ref[...] = total
    equal = jnp.sum(back_ref[...], axis=0, keepdims=True)
    place = lax.broadcasted_iota(jnp.int32, equal.shape, 1)
    departures_ref[...] = jnp.where(place < count_ref[0], innovation_ref[...] - equal, 0.0)


def per_device(
    perturbation,
    control,
    filter_length,
    modes,
    obs_weights,
    innovation,
    obs_tile,
    obs_column,
    obs_count,
):
    members, levels, rows, cols = perturbation.shape
    kinds = control.shape[1]
    lines = members * kinds
    n_mem, n_lat, n_lon = (lax.axis_size(a) for a in ("mem", "lat", "lon"))
    mem, lat, lon = (lax.axis_index(a) for a in ("mem", "lat", "lon"))
    slots = innovation.shape[0]
    share = levels // n_mem
    all_cols = cols * n_lon

    rate = jnp.exp(-1.0 / filter_length)
    rest = 1.0 - rate
    log = jnp.log1p(-rest)
    beta = rate * jnp.expm1(2.0 * rows * log) / jnp.expm1(2.0 * log)
    table = jnp.tile(jnp.stack([log, rate, beta], axis=1), (members, 1))
    lons = jnp.stack([source(lon, s, n_lon) for s in range(n_lon)]).astype(jnp.int32)

    def ends(place):
        reach = (all_cols - place * cols - jnp.arange(cols)).astype(F32)
        return (rest * rest)[:, None] * -jnp.expm1(2.0 * log[:, None] * reach[None, :])

    matrix = pl.pallas_call(
        matrix_kernel,
        out_shape=jax.ShapeDtypeStruct((kinds, all_cols, 2 * cols), BF16),
        in_specs=[SMEM, SMEM, VMEM, VMEM],
        out_specs=VMEM,
        **params(8 * kinds * all_cols * cols, 4 * kinds * all_cols * cols, 5 * kinds * all_cols * cols),
    )(
        lons * cols,
        log,
        ends(lon),
        jnp.stack([ends(source(lon, s, n_lon)).T for s in range(n_lon)]),
    )

    whole = control.astype(F32)
    others = [send(whole, "lon", s) for s in range(1, n_lon)]
    others = jnp.stack(others) if others else jnp.zeros((1,) + whole.shape, F32)
    field, edge = pl.pallas_call(
        columns_kernel,
        out_shape=(
            jax.ShapeDtypeStruct((rows * lines, cols), F32),
            jax.ShapeDtypeStruct((2, lines, cols), F32),
        ),
        in_specs=[VMEM] * 4,
        out_specs=(VMEM, VMEM),
        scratch_shapes=[pltpu.VMEM((rows * lines, cols), F32)],
        **params(
            4 * lines * rows * cols * all_cols,
            4 * 2**20,
            4 * lines * rows * (2 * cols + all_cols) + 4 * kinds * all_cols * cols,
        ),
    )(control, others, matrix, table)

    obs_weights, obs_tile, obs_column, _ = lax.optimization_barrier(
        (obs_weights, obs_tile, obs_column, edge)
    )
    valid = jnp.arange(slots, dtype=jnp.int32) < obs_count[0]
    target = obs_tile[:, 0]
    fine_row = target // n_lon * (2 * rows) + obs_column // (2 * cols)
    fine_col = target % n_lon * (2 * cols) + obs_column % (2 * cols)
    weights = jnp.where(valid[:, None], obs_weights.astype(F32), 0.0).T
    places = jnp.stack([fine_row, fine_col]).astype(F32)
    packed = jnp.concatenate([weights, places, jnp.zeros((6, slots), F32)])

    edges = edge[None]
    step = 1
    while step < n_lat and paired(n_lat):
        edges = jnp.concatenate([edges, send(edges, "lat", step)])
        if step == 1:
            packed = lax.optimization_barrier((packed, edges))[0]
        step *= 2
    if not paired(n_lat):
        edges = collect(edge, "lat")
    packed = [packed] + [send(packed, "lat", s) for s in range(1, n_lat)]
    lats = jnp.stack([source(lat, s, n_lat) for s in range(n_lat)]).astype(jnp.int32)
    chunks = jnp.stack([toward(mem, r, n_mem) for r in range(n_mem)]).astype(jnp.int32)
    chunk_shape = jax.ShapeDtypeStruct((share * rows, cols), F32)
    sums = pl.pallas_call(
        functools.partial(sum_kernel, 1.0 / math.sqrt(members * n_mem - 1)),
        out_shape=(chunk_shape,) * n_mem,
        in_specs=[SMEM, SMEM] + [VMEM] * 5,
        out_specs=(VMEM,) * n_mem,
        scratch_shapes=[
            pltpu.VMEM((rows * lines, cols), F32),
            pltpu.VMEM((3 * lines, rows * cols), BF16),
            pltpu.VMEM((members * levels * rows, cols), F32),
        ],
        **params(
            6 * members * levels * lines * rows * cols,
            6 * 2**20,
            (6 * members + 4) * levels * rows * cols + 14 * lines * rows * cols,
        ),
    )(lats, chunks, table, edges, field, modes, perturbation)


    tiles = n_lat * n_lon
    packed = jnp.stack(lax.optimization_barrier((packed, sums[0]))[0])
    packs = [packed] + [send(packed, "lon", s) for s in range(1, n_lon)]
    equal = pl.pallas_call(
        functools.partial(observe_kernel, levels, rows),
        out_shape=jax.ShapeDtypeStruct((n_mem * tiles, slots), F32),
        in_specs=[SMEM] * 3 + [VMEM] * (n_mem + n_lon),
        out_specs=VMEM,
        scratch_shapes=[pltpu.VMEM((levels * rows, 2 * cols), BF16)],
        **params(
            4 * levels * rows * cols * tiles * slots,
            4 * 2**20,
            8 * levels * rows * cols + packed.size * n_lon * 4 + n_mem * tiles * slots * 4,
        ),
    )(
        chunks,
        jnp.stack([lat * rows, lon * cols]).astype(jnp.int32),
        (lats[None, :] * n_lon + lons[:, None]).reshape(-1),
        *sums,
        *packs,
    )

    held, leaving = [[chunk] for chunk in sums], equal
    if paired(n_mem):
        step = 1
        while step < n_mem:
            for r in reversed(range(step, n_mem, 2 * step)):
                part = functools.reduce(jnp.add, held[r])
                if 2 * step == n_mem:
                    leaving = lax.optimization_barrier((equal, part))[0]
                got = send(part, "mem", step)
                if r == 3:
                    got, _ = lax.optimization_barrier((got, equal))
                held[r ^ step].append(got)
            step *= 2
    else:
        for r in range(1, n_mem):
            held[0].append(send(sums[r], "mem", r))
    back = lax.all_to_all(leaving, ("mem", "lat", "lon"), 0, 0, tiled=True)
    increment, departures = pl.pallas_call(
        finish_kernel,
        out_shape=(chunk_shape, jax.ShapeDtypeStruct((1, slots), F32)),
        in_specs=[SMEM] + [VMEM] * (2 + len(held[0])),
        out_specs=(VMEM, VMEM),
        **params(
            len(held[0]) * share * rows * cols,
            8 * len(held[0]) * share * rows * cols,
            8 * (len(held[0]) + 1) * share * rows * cols + 8 * n_mem * tiles * slots,
        ),
    )(obs_count, innovation[None], back, *held[0])
    increment, departures = increment.reshape(share, rows, cols), departures[0]
    return (increment, departures)


def solution(mesh):
    placed = (
        P("mem", None, "lat", "lon"),
        P("mem", None, "lat", "lon"),
        P(),
        P(),
        P(("lat", "lon"), None),
        P(("lat", "lon")),
        P(("lat", "lon"), None),
        P(("lat", "lon")),
        P(("lat", "lon")),
    )
    return jax.shard_map(
        per_device,
        mesh=mesh,
        in_specs=placed,
        out_specs=(P("mem", "lat", "lon"), P(("lat", "lon"))),
        check_vma=False,
    )
```

```python
import functools
import math

import jax
import jax.numpy as jnp
from jax import lax
from jax.experimental import pallas as pl
from jax.experimental.pallas import tpu as pltpu
from jax.sharding import PartitionSpec as P

F32, BF16 = jnp.float32, jnp.bfloat16
VMEM = pl.BlockSpec(memory_space=pltpu.VMEM)
SMEM = pl.BlockSpec(memory_space=pltpu.SMEM)


def params(flops, moved, held):
    return dict(
        compiler_params=pltpu.CompilerParams(vmem_limit_bytes=held + 2 * 2**20),
        cost_estimate=pl.CostEstimate(flops=flops, bytes_accessed=moved, transcendentals=0),
    )


def paired(count):
    return count & (count - 1) == 0


def toward(place, step, count):
    return place ^ step if paired(count) else (place + step) % count


def source(place, step, count):
    return place ^ step if paired(count) else (place - step) % count


def send(block, axis, step):
    count = lax.axis_size(axis)
    return lax.ppermute(block, axis, [(i, toward(i, step, count)) for i in range(count)])


def collect(block, axis):
    count = lax.axis_size(axis)
    blocks = block[None]
    if not paired(count):
        return jnp.concatenate([blocks] + [send(blocks, axis, s) for s in range(1, count)])
    step = 1
    while step < count:
        blocks = jnp.concatenate([blocks, send(blocks, axis, step)])
        step *= 2
    return blocks


def halve(value):
    high = value.astype(BF16)
    return high, (value - high.astype(F32)).astype(BF16)


def matrix_kernel(starts_ref, log_ref, to_ref, from_ref, matrix_ref):
    sources, cols, modes = from_ref.shape
    across = lax.broadcasted_iota(jnp.int32, (cols, cols), 1) + starts_ref[0]
    for s in range(sources):
        down = lax.broadcasted_iota(jnp.int32, (cols, cols), 0) + starts_ref[s]
        distance = jnp.abs(across - down).astype(F32)
        for k in range(modes):
            end = jnp.where(across >= down, to_ref[k : k + 1, :], from_ref[s, :, k : k + 1])
            high, low = halve(jnp.exp(distance * log_ref[k]) * end)
            at = s * cols
            matrix_ref[k, at : at + cols, :] = jnp.concatenate([high, low], axis=1)


def columns_kernel(own_ref, other_ref, matrix_ref, table_ref, field_ref, edge_ref, first):
    members, modes, rows, cols = own_ref.shape
    sources = matrix_ref.shape[1] // cols
    lines = members * modes
    pitch = field_ref.shape[0] // rows
    for k in range(modes):
        pieces = [jnp.concatenate([own_ref[m, k] for m in range(members)])]
        for s in range(1, sources):
            pieces.append(
                jnp.concatenate([other_ref[s - 1, m, k] for m in range(members)]).astype(BF16)
            )
        both = jnp.dot(
            jnp.concatenate(pieces, axis=1), matrix_ref[k], preferred_element_type=F32
        )
        made = both[:, :cols] + both[:, cols:]
        for m in range(members):
            field_ref[pl.ds(m * modes + k, rows, stride=pitch), :] = made[m * rows : (m + 1) * rows]
    decay = jnp.broadcast_to(table_ref[:, 1:2], (lines, cols))
    state = jnp.zeros((lines, cols), F32)
    for x in range(rows):
        state = decay * state + field_ref[x * pitch : x * pitch + lines, :]
        first[x * lines : (x + 1) * lines, :] = state
    edge_ref[0] = state
    state = jnp.zeros((lines, cols), F32)
    for x in reversed(range(rows)):
        state = decay * state + first[x * lines : (x + 1) * lines, :]
    edge_ref[1] = state


def sum_kernel(
    scale, places_ref, chunks_ref, table_ref, edges_ref, field_ref, modes_ref, pert_ref, *rest
):
    chunks = len(rest) - 4
    outs, (first, second, pert, turned) = rest[:chunks], rest[chunks:]
    members, levels, rows, cols = pert_ref.shape
    lines, kinds = table_ref.shape[0], table_ref.shape[0] // members
    share = levels // chunks
    count = edges_ref.shape[0]
    pitch = pert.shape[0] // (members * levels)
    field_pitch = field_ref.shape[0] // rows

    for m in range(members):
        for z in range(levels):
            at = (m * levels + z) * pitch
            pert[at : at + rows, :] = pert_ref[m, z].astype(F32)

    log, decay, beta = (
        jnp.broadcast_to(table_ref[:, i : i + 1], (lines, cols)) for i in range(3)
    )

    def power(ahead):
        exponent = (rows * jnp.maximum(ahead, 0)).astype(F32)
        return jnp.where(ahead >= 0, jnp.exp(log * exponent), 0.0)

    own = places_ref[0]
    state = jnp.zeros((lines, cols), F32)
    after = jnp.zeros((lines, cols), F32)
    for s in range(count):
        there = places_ref[s]
        state = state + power(own - there - 1) * edges_ref[s, 0]
        before = jnp.zeros((lines, cols), F32)
        for t in range(count):
            before = before + power(there - places_ref[t] - 1) * edges_ref[t, 0]
        after = after + power(there - own - 1) * (edges_ref[s, 1] + beta * before)

    for x in range(rows):
        state = decay * state + field_ref[x * field_pitch : x * field_pitch + lines, :]
        first[x * lines : (x + 1) * lines, :] = state
    state = after
    for x in reversed(range(rows)):
        state = decay * state + first[x * lines : (x + 1) * lines, :]
        high, low = halve(state)
        second[:, x * cols : (x + 1) * cols] = jnp.concatenate([high, low, high])

    turned[...] = (modes_ref[...] * scale).T
    held = jnp.concatenate([turned[pl.ds(chunks_ref[r] * share, share), :] for r in range(chunks)])
    held = jnp.concatenate([held] * members, axis=1)
    member = lax.broadcasted_iota(jnp.int32, (levels, lines), 1) // kinds
    high, low = halve(
        jnp.concatenate([jnp.where(member == m, held, 0.0) for m in range(members)])
    )
    weights = jnp.concatenate([high, high, low], axis=1)

    for pair in range(0, rows, 2):
        profile = jnp.dot(
            weights,
            second[:, pair * cols : (pair + 2) * cols],
            preferred_element_type=F32,
        )
        for half in range(2):
            x = pair + half
            for r in range(chunks):
                total = None
                for m in range(members):
                    at = (m * levels + chunks_ref[r] * share) * pitch + x
                    line = m * levels + r * share
                    term = (
                        profile[line : line + share, half * cols : (half + 1) * cols]
                        * pert[pl.ds(at, share, stride=pitch), :]
                    )
                    total = term if total is None else total + term
                outs[r][pl.ds(x, share, stride=rows), :] = total


def observe_kernel(levels, rows, chunks_ref, origin_ref, spots_ref, *rest):
    chunks, tiles = chunks_ref.shape[0], spots_ref.shape[0]
    sums, packs, (out_ref, split) = rest[:chunks], rest[chunks:-2], rest[-2:]
    slots = out_ref.shape[1]
    step, cols = sums[0].shape
    for r in range(chunks):
        high, low = halve(sums[r][...])
        at = pl.multiple_of(chunks_ref[r] * step, step)
        split[pl.ds(at, step), :] = jnp.concatenate([high, low], axis=1)

    def spread(fine, origin, length):
        near = jnp.floor(fine * 0.5)
        far = near - 1.0 + 2.0 * (fine - 2.0 * near)
        cell = (lax.broadcasted_iota(jnp.int32, (length, slots), 0) + origin).astype(F32)
        return jnp.where(cell == near, 0.75, 0.0) + jnp.where(cell == far, 0.25, 0.0)

    group = math.gcd(levels, 16)
    before = 0
    for packed_ref in packs:

        @pl.loop(0, packed_ref.shape[0])
        def _(block, packed_ref=packed_ref, before=before):
            fine = packed_ref[block, levels : levels + 8, :]
            across = spread(fine[1:2], origin_ref[1], cols).astype(BF16)
            across = jnp.concatenate([across, across])
            down = spread(fine[0:1], origin_ref[0], rows)
            total = jnp.zeros((rows, slots), F32)
            for g in range(0, levels, group):
                seen = jnp.dot(
                    split[g * rows : (g + group) * rows, :], across, preferred_element_type=F32
                )
                weights = packed_ref[block, g : g + group, :]
                for z in range(group):
                    total = total + seen[z * rows : (z + 1) * rows] * weights[z : z + 1]
            row = jnp.sum(total * down, axis=0, keepdims=True)
            for copy in range(out_ref.shape[0] // tiles):
                out_ref[pl.ds(copy * tiles + spots_ref[before + block], 1), :] = row

        before += packed_ref.shape[0]


def finish_kernel(count_ref, innovation_ref, back_ref, *rest):
    parts, (increment_ref, departures_ref) = rest[:-2], rest[-2:]
    total = parts[0][...]
    for part in parts[1:]:
        total = total + part[...]
    increment_ref[...] = total
    equal = jnp.sum(back_ref[...], axis=0, keepdims=True)
    place = lax.broadcasted_iota(jnp.int32, equal.shape, 1)
    departures_ref[...] = jnp.where(place < count_ref[0], innovation_ref[...] - equal, 0.0)


def per_device(
    perturbation,
    control,
    filter_length,
    modes,
    obs_weights,
    innovation,
    obs_tile,
    obs_column,
    obs_count,
):
    members, levels, rows, cols = perturbation.shape
    kinds = control.shape[1]
    lines = members * kinds
    n_mem, n_lat, n_lon = (lax.axis_size(a) for a in ("mem", "lat", "lon"))
    mem, lat, lon = (lax.axis_index(a) for a in ("mem", "lat", "lon"))
    slots = innovation.shape[0]
    share = levels // n_mem
    all_cols = cols * n_lon

    rate = jnp.exp(-1.0 / filter_length)
    rest = 1.0 - rate
    log = jnp.log1p(-rest)
    beta = rate * jnp.expm1(2.0 * rows * log) / jnp.expm1(2.0 * log)
    table = jnp.tile(jnp.stack([log, rate, beta], axis=1), (members, 1))
    lons = jnp.stack([source(lon, s, n_lon) for s in range(n_lon)]).astype(jnp.int32)

    def ends(place):
        reach = (all_cols - place * cols - jnp.arange(cols)).astype(F32)
        return (rest * rest)[:, None] * -jnp.expm1(2.0 * log[:, None] * reach[None, :])

    matrix = pl.pallas_call(
        matrix_kernel,
        out_shape=jax.ShapeDtypeStruct((kinds, all_cols, 2 * cols), BF16),
        in_specs=[SMEM, SMEM, VMEM, VMEM],
        out_specs=VMEM,
        **params(8 * kinds * all_cols * cols, 4 * kinds * all_cols * cols, 5 * kinds * all_cols * cols),
    )(
        lons * cols,
        log,
        ends(lon),
        jnp.stack([ends(source(lon, s, n_lon)).T for s in range(n_lon)]),
    )

    whole = control.astype(F32)
    others = [send(whole, "lon", s) for s in range(1, n_lon)]
    others = jnp.stack(others) if others else jnp.zeros((1,) + whole.shape, F32)
    field, edge = pl.pallas_call(
        columns_kernel,
        out_shape=(
            jax.ShapeDtypeStruct((rows * (lines + 8), cols), F32),
            jax.ShapeDtypeStruct((2, lines, cols), F32),
        ),
        in_specs=[VMEM] * 4,
        out_specs=(VMEM, VMEM),
        scratch_shapes=[pltpu.VMEM((rows * lines, cols), F32)],
        **params(
            4 * lines * rows * cols * all_cols,
            4 * 2**20,
            4 * lines * rows * (2 * cols + all_cols) + 4 * kinds * all_cols * cols,
        ),
    )(control, others, matrix, table)

    obs_weights, obs_tile, obs_column, _ = lax.optimization_barrier(
        (obs_weights, obs_tile, obs_column, edge)
    )
    valid = jnp.arange(slots, dtype=jnp.int32) < obs_count[0]
    target = obs_tile[:, 0]
    fine_row = target // n_lon * (2 * rows) + obs_column // (2 * cols)
    fine_col = target % n_lon * (2 * cols) + obs_column % (2 * cols)
    weights = jnp.where(valid[:, None], obs_weights.astype(F32), 0.0).T
    places = jnp.stack([fine_row, fine_col]).astype(F32)
    packed = jnp.concatenate([weights, places, jnp.zeros((6, slots), F32)])

    edges = edge[None]
    step = 1
    while step < n_lat and paired(n_lat):
        edges = jnp.concatenate([edges, send(edges, "lat", step)])
        if step == 1:
            packed = lax.optimization_barrier((packed, edges))[0]
        step *= 2
    if not paired(n_lat):
        edges = collect(edge, "lat")
    packed = [packed] + [send(packed, "lat", s) for s in range(1, n_lat)]
    lats = jnp.stack([source(lat, s, n_lat) for s in range(n_lat)]).astype(jnp.int32)
    chunks = jnp.stack([toward(mem, r, n_mem) for r in range(n_mem)]).astype(jnp.int32)
    chunk_shape = jax.ShapeDtypeStruct((share * rows, cols), F32)
    sums = pl.pallas_call(
        functools.partial(sum_kernel, 1.0 / math.sqrt(members * n_mem - 1)),
        out_shape=(chunk_shape,) * n_mem,
        in_specs=[SMEM, SMEM] + [VMEM] * 5,
        out_specs=(VMEM,) * n_mem,
        scratch_shapes=[
            pltpu.VMEM((rows * lines, cols), F32),
            pltpu.VMEM((3 * lines, rows * cols), BF16),
            pltpu.VMEM((members * levels * (rows + 4), cols), F32),
            pltpu.VMEM((levels, kinds), F32),
        ],
        **params(
            6 * members * levels * lines * rows * cols,
            6 * 2**20,
            (7 * members + 4) * levels * rows * cols + 14 * lines * rows * cols,
        ),
    )(lats, chunks, table, edges, field, modes.T, perturbation)


    tiles = n_lat * n_lon
    packed = jnp.stack(lax.optimization_barrier((packed, sums[0]))[0])
    packs = [packed] + [send(packed, "lon", s) for s in range(1, n_lon)]
    equal = pl.pallas_call(
        functools.partial(observe_kernel, levels, rows),
        out_shape=jax.ShapeDtypeStruct((n_mem * tiles, slots), F32),
        in_specs=[SMEM] * 3 + [VMEM] * (n_mem + n_lon),
        out_specs=VMEM,
        scratch_shapes=[pltpu.VMEM((levels * rows, 2 * cols), BF16)],
        **params(
            4 * levels * rows * cols * tiles * slots,
            4 * 2**20,
            8 * levels * rows * cols + packed.size * n_lon * 4 + n_mem * tiles * slots * 4,
        ),
    )(
        chunks,
        jnp.stack([lat * rows, lon * cols]).astype(jnp.int32),
        (lats[None, :] * n_lon + lons[:, None]).reshape(-1),
        *sums,
        *packs,
    )

    held, leaving = [[chunk] for chunk in sums], equal
    if paired(n_mem):
        step = 1
        while step < n_mem:
            for r in reversed(range(step, n_mem, 2 * step)):
                part = functools.reduce(jnp.add, held[r])
                if 2 * step == n_mem:
                    leaving = lax.optimization_barrier((equal, part))[0]
                got = send(part, "mem", step)
                if r == 3:
                    got, _ = lax.optimization_barrier((got, equal))
                held[r ^ step].append(got)
            step *= 2
    else:
        for r in range(1, n_mem):
            held[0].append(send(sums[r], "mem", r))
    back = lax.all_to_all(leaving, ("mem", "lat", "lon"), 0, 0, tiled=True)
    increment, departures = pl.pallas_call(
        finish_kernel,
        out_shape=(chunk_shape, jax.ShapeDtypeStruct((1, slots), F32)),
        in_specs=[SMEM] + [VMEM] * (2 + len(held[0])),
        out_specs=(VMEM, VMEM),
        **params(
            len(held[0]) * share * rows * cols,
            8 * len(held[0]) * share * rows * cols,
            8 * (len(held[0]) + 1) * share * rows * cols + 8 * n_mem * tiles * slots,
        ),
    )(obs_count, innovation[None], back, *held[0])
    increment, departures = increment.reshape(share, rows, cols), departures[0]
    return (increment, departures)


def solution(mesh):
    placed = (
        P("mem", None, "lat", "lon"),
        P("mem", None, "lat", "lon"),
        P(),
        P(),
        P(("lat", "lon"), None),
        P(("lat", "lon")),
        P(("lat", "lon"), None),
        P(("lat", "lon")),
        P(("lat", "lon")),
    )
    return jax.shard_map(
        per_device,
        mesh=mesh,
        in_specs=placed,
        out_specs=(P("mem", "lat", "lon"), P(("lat", "lon"))),
        check_vma=False,
    )
```

```python
import functools
import math

import jax
import jax.numpy as jnp
from jax import lax
from jax.experimental import pallas as pl
from jax.experimental.pallas import tpu as pltpu
from jax.sharding import PartitionSpec as P

F32, BF16 = jnp.float32, jnp.bfloat16
VMEM = pl.BlockSpec(memory_space=pltpu.VMEM)
SMEM = pl.BlockSpec(memory_space=pltpu.SMEM)


def params(flops, moved, held):
    return dict(
        compiler_params=pltpu.CompilerParams(vmem_limit_bytes=held + 2 * 2**20),
        cost_estimate=pl.CostEstimate(flops=flops, bytes_accessed=moved, transcendentals=0),
    )


def paired(count):
    return count & (count - 1) == 0


def toward(place, step, count):
    return place ^ step if paired(count) else (place + step) % count


def source(place, step, count):
    return place ^ step if paired(count) else (place - step) % count


def send(block, axis, step):
    count = lax.axis_size(axis)
    return lax.ppermute(block, axis, [(i, toward(i, step, count)) for i in range(count)])


def collect(block, axis):
    count = lax.axis_size(axis)
    blocks = block[None]
    if not paired(count):
        return jnp.concatenate([blocks] + [send(blocks, axis, s) for s in range(1, count)])
    step = 1
    while step < count:
        blocks = jnp.concatenate([blocks, send(blocks, axis, step)])
        step *= 2
    return blocks


def halve(value):
    high = value.astype(BF16)
    return high, (value - high.astype(F32)).astype(BF16)


def matrix_kernel(starts_ref, log_ref, to_ref, from_ref, matrix_ref):
    sources, cols, modes = from_ref.shape
    across = lax.broadcasted_iota(jnp.int32, (cols, cols), 1) + starts_ref[0]
    for s in range(sources):
        down = lax.broadcasted_iota(jnp.int32, (cols, cols), 0) + starts_ref[s]
        distance = jnp.abs(across - down).astype(F32)
        for k in range(modes):
            end = jnp.where(across >= down, to_ref[k : k + 1, :], from_ref[s, :, k : k + 1])
            high, low = halve(jnp.exp(distance * log_ref[k : k + 1, :1]) * end)
            at = s * cols
            matrix_ref[k, at : at + cols, :] = jnp.concatenate([high, low], axis=1)


def columns_kernel(own_ref, other_ref, matrix_ref, table_ref, field_ref, edge_ref, first):
    members, modes, rows, cols = own_ref.shape
    sources = matrix_ref.shape[1] // cols
    lines = members * modes
    pitch = field_ref.shape[0] // rows
    for k in range(modes):
        pieces = [jnp.concatenate([own_ref[m, k] for m in range(members)])]
        for s in range(1, sources):
            pieces.append(
                jnp.concatenate([other_ref[s - 1, m, k] for m in range(members)]).astype(BF16)
            )
        both = jnp.dot(
            jnp.concatenate(pieces, axis=1), matrix_ref[k], preferred_element_type=F32
        )
        made = both[:, :cols] + both[:, cols:]
        for m in range(members):
            field_ref[pl.ds(m * modes + k, rows, stride=pitch), :] = made[m * rows : (m + 1) * rows]
    decay = jnp.broadcast_to(table_ref[:, 1:2], (lines, cols))
    state = jnp.zeros((lines, cols), F32)
    for x in range(rows):
        state = decay * state + field_ref[x * pitch : x * pitch + lines, :]
        first[x * lines : (x + 1) * lines, :] = state
    edge_ref[0] = state
    state = jnp.zeros((lines, cols), F32)
    for x in reversed(range(rows)):
        state = decay * state + first[x * lines : (x + 1) * lines, :]
    edge_ref[1] = state


def sum_kernel(
    scale, places_ref, chunks_ref, table_ref, edges_ref, field_ref, modes_ref, pert_ref, *rest
):
    chunks = len(rest) - 4
    outs, (first, second, pert, turned) = rest[:chunks], rest[chunks:]
    members, levels, rows, cols = pert_ref.shape
    lines, kinds = table_ref.shape[0], table_ref.shape[0] // members
    share = levels // chunks
    count = edges_ref.shape[0]
    pitch = pert.shape[0] // (members * levels)
    field_pitch = field_ref.shape[0] // rows

    for m in range(members):
        for z in range(levels):
            at = (m * levels + z) * pitch
            pert[at : at + rows, :] = pert_ref[m, z].astype(F32)

    log, decay, beta = (
        jnp.broadcast_to(table_ref[:, i : i + 1], (lines, cols)) for i in range(3)
    )

    def power(ahead):
        exponent = (rows * jnp.maximum(ahead, 0)).astype(F32)
        return jnp.where(ahead >= 0, jnp.exp(log * exponent), 0.0)

    own = places_ref[0]
    state = jnp.zeros((lines, cols), F32)
    after = jnp.zeros((lines, cols), F32)
    for s in range(count):
        there = places_ref[s]
        state = state + power(own - there - 1) * edges_ref[s, 0]
        before = jnp.zeros((lines, cols), F32)
        for t in range(count):
            before = before + power(there - places_ref[t] - 1) * edges_ref[t, 0]
        after = after + power(there - own - 1) * (edges_ref[s, 1] + beta * before)

    for x in range(rows):
        state = decay * state + field_ref[x * field_pitch : x * field_pitch + lines, :]
        first[x * lines : (x + 1) * lines, :] = state
    state = after
    for x in reversed(range(rows)):
        state = decay * state + first[x * lines : (x + 1) * lines, :]
        high, low = halve(state)
        second[:, x * cols : (x + 1) * cols] = jnp.concatenate([high, low, high])

    turned[...] = (modes_ref[...] * scale).T
    held = jnp.concatenate([turned[pl.ds(chunks_ref[r] * share, share), :] for r in range(chunks)])
    held = jnp.concatenate([held] * members, axis=1)
    member = lax.broadcasted_iota(jnp.int32, (levels, lines), 1) // kinds
    high, low = halve(
        jnp.concatenate([jnp.where(member == m, held, 0.0) for m in range(members)])
    )
    weights = jnp.concatenate([high, high, low], axis=1)

    for pair in range(0, rows, 2):
        profile = jnp.dot(
            weights,
            second[:, pair * cols : (pair + 2) * cols],
            preferred_element_type=F32,
        )
        for half in range(2):
            x = pair + half
            for r in range(chunks):
                total = None
                for m in range(members):
                    at = (m * levels + chunks_ref[r] * share) * pitch + x
                    line = m * levels + r * share
                    term = (
                        profile[line : line + share, half * cols : (half + 1) * cols]
                        * pert[pl.ds(at, share, stride=pitch), :]
                    )
                    total = term if total is None else total + term
                outs[r][pl.ds(x, share, stride=rows), :] = total


def observed(levels, rows, origin_ref, packed_ref, block, split):
    slots, cols = packed_ref.shape[2], split.shape[1] // 2

    def spread(fine, origin, length):
        near = jnp.floor(fine * 0.5)
        far = near - 1.0 + 2.0 * (fine - 2.0 * near)
        cell = (lax.broadcasted_iota(jnp.int32, (length, slots), 0) + origin).astype(F32)
        return jnp.where(cell == near, 0.75, 0.0) + jnp.where(cell == far, 0.25, 0.0)

    group = math.gcd(levels, 16)
    fine = packed_ref[block, levels : levels + 8, :]
    across = spread(fine[1:2], origin_ref[1], cols).astype(BF16)
    across = jnp.concatenate([across, across])
    down = spread(fine[0:1], origin_ref[0], rows)
    total = jnp.zeros((rows, slots), F32)
    for g in range(0, levels, group):
        seen = jnp.dot(
            split[g * rows : (g + group) * rows, :], across, preferred_element_type=F32
        )
        weights = packed_ref[block, g : g + group, :]
        for z in range(group):
            total = total + seen[z * rows : (z + 1) * rows] * weights[z : z + 1]
    return jnp.sum(total * down, axis=0, keepdims=True)


def near_kernel(levels, rows, chunks_ref, origin_ref, *rest):
    chunks = chunks_ref.shape[0]
    sums, packs, (out_ref, split) = rest[:chunks], rest[chunks:-2], rest[-2:]
    step = sums[0].shape[0]
    for r in range(chunks):
        high, low = halve(sums[r][...])
        at = pl.multiple_of(chunks_ref[r] * step, step)
        split[pl.ds(at, step), :] = jnp.concatenate([high, low], axis=1)
    for i, packed_ref in enumerate(packs):
        out_ref[i : i + 1, :] = observed(levels, rows, origin_ref, packed_ref, 0, split)


def far_kernel(levels, rows, origin_ref, spots_ref, split, near_ref, *rest):
    packs, out_ref = rest[:-1], rest[-1]
    tiles = spots_ref.shape[0]

    def put(place, row):
        for copy in range(out_ref.shape[0] // tiles):
            out_ref[pl.ds(copy * tiles + spots_ref[place], 1), :] = row

    before = near_ref.shape[0]
    for i in range(before):
        put(i, near_ref[i : i + 1, :])
    for packed_ref in packs:

        @pl.loop(0, packed_ref.shape[0])
        def _(block, packed_ref=packed_ref, before=before):
            put(before + block, observed(levels, rows, origin_ref, packed_ref, block, split))

        before += packed_ref.shape[0]


def finish_kernel(count_ref, innovation_ref, back_ref, *rest):
    parts, (increment_ref, departures_ref) = rest[:-2], rest[-2:]
    total = parts[0][...]
    for part in parts[1:]:
        total = total + part[...]
    increment_ref[...] = total
    equal = jnp.sum(back_ref[...], axis=0, keepdims=True)
    place = lax.broadcasted_iota(jnp.int32, equal.shape, 1)
    departures_ref[...] = jnp.where(place < count_ref[0], innovation_ref[...] - equal, 0.0)


def per_device(
    perturbation,
    control,
    filter_length,
    modes,
    obs_weights,
    innovation,
    obs_tile,
    obs_column,
    obs_count,
):
    members, levels, rows, cols = perturbation.shape
    kinds = control.shape[1]
    lines = members * kinds
    n_mem, n_lat, n_lon = (lax.axis_size(a) for a in ("mem", "lat", "lon"))
    mem, lat, lon = (lax.axis_index(a) for a in ("mem", "lat", "lon"))
    slots = innovation.shape[0]
    share = levels // n_mem
    all_cols = cols * n_lon

    rate = jnp.exp(-1.0 / filter_length)
    rest = 1.0 - rate
    log = jnp.log1p(-rest)
    beta = rate * jnp.expm1(2.0 * rows * log) / jnp.expm1(2.0 * log)
    table = jnp.tile(jnp.stack([log, rate, beta], axis=1), (members, 1))
    lons = jnp.stack([source(lon, s, n_lon) for s in range(n_lon)]).astype(jnp.int32)

    def ends(place):
        reach = (all_cols - place * cols - jnp.arange(cols)).astype(F32)
        return (rest * rest)[:, None] * -jnp.expm1(2.0 * log[:, None] * reach[None, :])

    matrix = pl.pallas_call(
        matrix_kernel,
        out_shape=jax.ShapeDtypeStruct((kinds, all_cols, 2 * cols), BF16),
        in_specs=[SMEM, VMEM, VMEM, VMEM],
        out_specs=VMEM,
        **params(8 * kinds * all_cols * cols, 4 * kinds * all_cols * cols, 5 * kinds * all_cols * cols),
    )(
        lons * cols,
        log[:, None],
        ends(lon),
        jnp.stack([ends(source(lon, s, n_lon)).T for s in range(n_lon)]),
    )

    whole = control.astype(F32)
    others = [send(whole, "lon", s) for s in range(1, n_lon)]
    others = jnp.stack(others) if others else jnp.zeros((1,) + whole.shape, F32)
    field, edge = pl.pallas_call(
        columns_kernel,
        out_shape=(
            jax.ShapeDtypeStruct((rows * (lines + 8), cols), F32),
            jax.ShapeDtypeStruct((2, lines, cols), F32),
        ),
        in_specs=[VMEM] * 4,
        out_specs=(VMEM, VMEM),
        scratch_shapes=[pltpu.VMEM((rows * lines, cols), F32)],
        **params(
            4 * lines * rows * cols * all_cols,
            4 * 2**20,
            4 * lines * rows * (2 * cols + all_cols) + 4 * kinds * all_cols * cols,
        ),
    )(control, others, matrix, table)

    obs_weights, obs_tile, obs_column, _ = lax.optimization_barrier(
        (obs_weights, obs_tile, obs_column, edge)
    )
    valid = jnp.arange(slots, dtype=jnp.int32) < obs_count[0]
    target = obs_tile[:, 0]
    fine_row = target // n_lon * (2 * rows) + obs_column // (2 * cols)
    fine_col = target % n_lon * (2 * cols) + obs_column % (2 * cols)
    weights = jnp.where(valid[:, None], obs_weights.astype(F32), 0.0).T
    places = jnp.stack([fine_row, fine_col]).astype(F32)
    packed = jnp.concatenate([weights, places, jnp.zeros((6, slots), F32)])

    edges = [edge] + [send(edge, "lat", s) for s in range(1, n_lat)]
    near = [packed[None]] + [send(packed[None], "lon", s) for s in range(1, n_lon)]
    edges = jnp.stack(edges)
    packed = [send(packed, "lat", s) for s in range(1, n_lat)]
    lats = jnp.stack([source(lat, s, n_lat) for s in range(n_lat)]).astype(jnp.int32)
    chunks = jnp.stack([toward(mem, r, n_mem) for r in range(n_mem)]).astype(jnp.int32)
    chunk_shape = jax.ShapeDtypeStruct((share * rows, cols), F32)
    sums = pl.pallas_call(
        functools.partial(sum_kernel, 1.0 / math.sqrt(members * n_mem - 1)),
        out_shape=(chunk_shape,) * n_mem,
        in_specs=[SMEM, SMEM] + [VMEM] * 5,
        out_specs=(VMEM,) * n_mem,
        scratch_shapes=[
            pltpu.VMEM((rows * lines, cols), F32),
            pltpu.VMEM((3 * lines, rows * cols), BF16),
            pltpu.VMEM((members * levels * (rows + 4), cols), F32),
            pltpu.VMEM((levels, kinds), F32),
        ],
        **params(
            6 * members * levels * lines * rows * cols,
            6 * 2**20,
            (7 * members + 4) * levels * rows * cols + 14 * lines * rows * cols,
        ),
    )(lats, chunks, table, edges, field, modes.T, perturbation)


    tiles = n_lat * n_lon
    origin = jnp.stack([lat * rows, lon * cols]).astype(jnp.int32)
    block_flops, block_size = 2 * levels * rows * cols * slots, 4 * (levels + 8) * slots
    equal, split = pl.pallas_call(
        functools.partial(near_kernel, levels, rows),
        out_shape=(
            jax.ShapeDtypeStruct((n_lon, slots), F32),
            jax.ShapeDtypeStruct((levels * rows, 2 * cols), BF16),
        ),
        in_specs=[SMEM] * 2 + [VMEM] * (n_mem + n_lon),
        out_specs=(VMEM, VMEM),
        **params(
            n_lon * block_flops, 2**20, 8 * levels * rows * cols + n_lon * block_size
        ),
    )(chunks, origin, *sums, *near)
    packs = []
    if n_lat > 1:
        packed = jnp.stack(lax.optimization_barrier((packed, equal))[0])
        packs = [packed] + [send(packed, "lon", s) for s in range(1, n_lon)]
    equal = pl.pallas_call(
        functools.partial(far_kernel, levels, rows),
        out_shape=jax.ShapeDtypeStruct((n_mem * tiles, slots), F32),
        in_specs=[SMEM] * 2 + [VMEM] * (2 + len(packs)),
        out_specs=VMEM,
        **params(
            (tiles - n_lon) * block_flops,
            4 * 2**20,
            4 * levels * rows * cols + tiles * block_size + n_mem * tiles * slots * 4,
        ),
    )(
        origin,
        jnp.concatenate(
            [lats[0] * n_lon + lons, (lats[None, 1:] * n_lon + lons[:, None]).reshape(-1)]
        ),
        split,
        equal,
        *packs,
    )

    held, leaving = [[chunk] for chunk in sums], equal
    if paired(n_mem):
        step = 1
        while step < n_mem:
            for r in reversed(range(step, n_mem, 2 * step)):
                part = functools.reduce(jnp.add, held[r])
                if 2 * step == n_mem:
                    leaving = lax.optimization_barrier((equal, part))[0]
                got = send(part, "mem", step)
                if r == 3:
                    got, _ = lax.optimization_barrier((got, equal))
                held[r ^ step].append(got)
            step *= 2
    else:
        for r in range(1, n_mem):
            held[0].append(send(sums[r], "mem", r))
    back = lax.all_to_all(leaving, ("mem", "lat", "lon"), 0, 0, tiled=True)
    increment, departures = pl.pallas_call(
        finish_kernel,
        out_shape=(chunk_shape, jax.ShapeDtypeStruct((1, slots), F32)),
        in_specs=[SMEM] + [VMEM] * (2 + len(held[0])),
        out_specs=(VMEM, VMEM),
        **params(
            len(held[0]) * share * rows * cols,
            8 * len(held[0]) * share * rows * cols,
            8 * (len(held[0]) + 1) * share * rows * cols + 8 * n_mem * tiles * slots,
        ),
    )(obs_count, innovation[None], back, *held[0])
    increment, departures = increment.reshape(share, rows, cols), departures[0]
    return (increment, departures)


def solution(mesh):
    placed = (
        P("mem", None, "lat", "lon"),
        P("mem", None, "lat", "lon"),
        P(),
        P(),
        P(("lat", "lon"), None),
        P(("lat", "lon")),
        P(("lat", "lon"), None),
        P(("lat", "lon")),
        P(("lat", "lon")),
    )
    return jax.shard_map(
        per_device,
        mesh=mesh,
        in_specs=placed,
        out_specs=(P("mem", "lat", "lon"), P(("lat", "lon"))),
        check_vma=False,
    )
```

```python
import functools
import math

import jax
import jax.numpy as jnp
from jax import lax
from jax.experimental import pallas as pl
from jax.experimental.pallas import tpu as pltpu
from jax.sharding import PartitionSpec as P

F32, BF16 = jnp.float32, jnp.bfloat16
VMEM = pl.BlockSpec(memory_space=pltpu.VMEM)
SMEM = pl.BlockSpec(memory_space=pltpu.SMEM)


def params(flops, moved, held):
    return dict(
        compiler_params=pltpu.CompilerParams(vmem_limit_bytes=held + 2 * 2**20),
        cost_estimate=pl.CostEstimate(flops=flops, bytes_accessed=moved, transcendentals=0),
    )


def paired(count):
    return count & (count - 1) == 0


def toward(place, step, count):
    return place ^ step if paired(count) else (place + step) % count


def source(place, step, count):
    return place ^ step if paired(count) else (place - step) % count


def send(block, axis, step):
    count = lax.axis_size(axis)
    return lax.ppermute(block, axis, [(i, toward(i, step, count)) for i in range(count)])


def collect(block, axis):
    count = lax.axis_size(axis)
    blocks = block[None]
    if not paired(count):
        return jnp.concatenate([blocks] + [send(blocks, axis, s) for s in range(1, count)])
    step = 1
    while step < count:
        blocks = jnp.concatenate([blocks, send(blocks, axis, step)])
        step *= 2
    return blocks


def halve(value):
    high = value.astype(BF16)
    return high, (value - high.astype(F32)).astype(BF16)


def matrix_kernel(starts_ref, log_ref, log_row_ref, to_ref, from_ref, matrix_ref):
    sources, cols, modes = from_ref.shape
    own = starts_ref[0]

    def put(s, k, value):
        high, low = halve(value)
        matrix_ref[k, s * cols : (s + 1) * cols, :] = jnp.concatenate([high, low], axis=1)

    across = lax.broadcasted_iota(jnp.int32, (cols, cols), 1)
    down = lax.broadcasted_iota(jnp.int32, (cols, cols), 0)
    distance = jnp.abs(across - down).astype(F32)
    for k in range(modes):
        end = jnp.where(across >= down, to_ref[k : k + 1, :], from_ref[0, :, k : k + 1])
        put(0, k, jnp.exp(distance * log_ref[k : k + 1, :1]) * end)
    for s in range(1, sources):
        there = starts_ref[s]
        between = jnp.maximum(own, there)
        before = there < own
        row = own + lax.broadcasted_iota(jnp.int32, (modes, cols), 1) - between
        row = jnp.exp(jnp.abs(row).astype(F32) * log_ref[...])
        row = row * jnp.where(before, to_ref[...], 1.0)
        column = there + lax.broadcasted_iota(jnp.int32, (cols, modes), 0) - between
        column = jnp.exp(jnp.abs(column).astype(F32) * log_row_ref[...])
        column = column * jnp.where(before, 1.0, from_ref[s])
        for k in range(modes):
            put(s, k, column[:, k : k + 1] * row[k : k + 1, :])


def columns_kernel(own_ref, other_ref, matrix_ref, table_ref, field_ref, edge_ref, first):
    members, modes, rows, cols = own_ref.shape
    sources = matrix_ref.shape[1] // cols
    lines = members * modes
    pitch = field_ref.shape[0] // rows
    for k in range(modes):
        pieces = [jnp.concatenate([own_ref[m, k] for m in range(members)])]
        for s in range(1, sources):
            pieces.append(
                jnp.concatenate([other_ref[s - 1, m, k] for m in range(members)]).astype(BF16)
            )
        both = jnp.dot(
            jnp.concatenate(pieces, axis=1), matrix_ref[k], preferred_element_type=F32
        )
        made = both[:, :cols] + both[:, cols:]
        for m in range(members):
            field_ref[pl.ds(m * modes + k, rows, stride=pitch), :] = made[m * rows : (m + 1) * rows]
    decay = jnp.broadcast_to(table_ref[:, 1:2], (lines, cols))
    state = jnp.zeros((lines, cols), F32)
    for x in range(rows):
        state = decay * state + field_ref[x * pitch : x * pitch + lines, :]
        first[x * lines : (x + 1) * lines, :] = state
    edge_ref[0] = state
    state = jnp.zeros((lines, cols), F32)
    for x in reversed(range(rows)):
        state = decay * state + first[x * lines : (x + 1) * lines, :]
    edge_ref[1] = state


def sum_kernel(
    scale, places_ref, chunks_ref, table_ref, edges_ref, field_ref, modes_ref, pert_ref, *rest
):
    chunks = len(rest) - 4
    outs, (first, second, pert, turned) = rest[:chunks], rest[chunks:]
    members, levels, rows, cols = pert_ref.shape
    lines, kinds = table_ref.shape[0], table_ref.shape[0] // members
    share = levels // chunks
    count = edges_ref.shape[0]
    pitch = pert.shape[0] // (members * levels)
    field_pitch = field_ref.shape[0] // rows

    for m in range(members):
        for z in range(levels):
            at = (m * levels + z) * pitch
            pert[at : at + rows, :] = pert_ref[m, z].astype(F32)

    log, decay, beta = (
        jnp.broadcast_to(table_ref[:, i : i + 1], (lines, cols)) for i in range(3)
    )

    def power(ahead):
        exponent = (rows * jnp.maximum(ahead, 0)).astype(F32)
        return jnp.where(ahead >= 0, jnp.exp(log * exponent), 0.0)

    own = places_ref[0]
    state = jnp.zeros((lines, cols), F32)
    after = jnp.zeros((lines, cols), F32)
    for s in range(count):
        there = places_ref[s]
        state = state + power(own - there - 1) * edges_ref[s, 0]
        before = jnp.zeros((lines, cols), F32)
        for t in range(count):
            before = before + power(there - places_ref[t] - 1) * edges_ref[t, 0]
        after = after + power(there - own - 1) * (edges_ref[s, 1] + beta * before)

    for x in range(rows):
        state = decay * state + field_ref[x * field_pitch : x * field_pitch + lines, :]
        first[x * lines : (x + 1) * lines, :] = state
    state = after
    for x in reversed(range(rows)):
        state = decay * state + first[x * lines : (x + 1) * lines, :]
        high, low = halve(state)
        second[:, x * cols : (x + 1) * cols] = jnp.concatenate([high, low, high])

    turned[...] = (modes_ref[...] * scale).T
    held = jnp.concatenate([turned[pl.ds(chunks_ref[r] * share, share), :] for r in range(chunks)])
    held = jnp.concatenate([held] * members, axis=1)
    member = lax.broadcasted_iota(jnp.int32, (levels, lines), 1) // kinds
    high, low = halve(
        jnp.concatenate([jnp.where(member == m, held, 0.0) for m in range(members)])
    )
    weights = jnp.concatenate([high, high, low], axis=1)

    for pair in range(0, rows, 2):
        profile = jnp.dot(
            weights,
            second[:, pair * cols : (pair + 2) * cols],
            preferred_element_type=F32,
        )
        for half in range(2):
            x = pair + half
            for r in range(chunks):
                total = None
                for m in range(members):
                    at = (m * levels + chunks_ref[r] * share) * pitch + x
                    line = m * levels + r * share
                    term = (
                        profile[line : line + share, half * cols : (half + 1) * cols]
                        * pert[pl.ds(at, share, stride=pitch), :]
                    )
                    total = term if total is None else total + term
                outs[r][pl.ds(x, share, stride=rows), :] = total


def observed(levels, rows, origin_ref, packed_ref, block, split):
    slots, cols = packed_ref.shape[2], split.shape[1] // 2

    def spread(fine, origin, length):
        near = jnp.floor(fine * 0.5)
        far = near - 1.0 + 2.0 * (fine - 2.0 * near)
        cell = (lax.broadcasted_iota(jnp.int32, (length, slots), 0) + origin).astype(F32)
        return jnp.where(cell == near, 0.75, 0.0) + jnp.where(cell == far, 0.25, 0.0)

    group = math.gcd(levels, 16)
    fine = packed_ref[block, levels : levels + 8, :]
    across = spread(fine[1:2], origin_ref[1], cols).astype(BF16)
    across = jnp.concatenate([across, across])
    down = spread(fine[0:1], origin_ref[0], rows)
    total = jnp.zeros((rows, slots), F32)
    for g in range(0, levels, group):
        seen = jnp.dot(
            split[g * rows : (g + group) * rows, :], across, preferred_element_type=F32
        )
        weights = packed_ref[block, g : g + group, :]
        for z in range(group):
            total = total + seen[z * rows : (z + 1) * rows] * weights[z : z + 1]
    return jnp.sum(total * down, axis=0, keepdims=True)


def near_kernel(levels, rows, chunks_ref, origin_ref, *rest):
    chunks = chunks_ref.shape[0]
    sums, packs, (out_ref, split) = rest[:chunks], rest[chunks:-2], rest[-2:]
    step = sums[0].shape[0]
    for r in range(chunks):
        high, low = halve(sums[r][...])
        at = pl.multiple_of(chunks_ref[r] * step, step)
        split[pl.ds(at, step), :] = jnp.concatenate([high, low], axis=1)
    for i, packed_ref in enumerate(packs):
        out_ref[i : i + 1, :] = observed(levels, rows, origin_ref, packed_ref, 0, split)


def far_kernel(levels, rows, origin_ref, spots_ref, split, near_ref, *rest):
    packs, out_ref = rest[:-1], rest[-1]
    tiles = spots_ref.shape[0]

    def put(place, row):
        for copy in range(out_ref.shape[0] // tiles):
            out_ref[pl.ds(copy * tiles + spots_ref[place], 1), :] = row

    before = near_ref.shape[0]
    for i in range(before):
        put(i, near_ref[i : i + 1, :])
    for packed_ref in packs:

        @pl.loop(0, packed_ref.shape[0])
        def _(block, packed_ref=packed_ref, before=before):
            put(before + block, observed(levels, rows, origin_ref, packed_ref, block, split))

        before += packed_ref.shape[0]


def finish_kernel(valid_ref, innovation_ref, back_ref, *rest):
    parts, (increment_ref, departures_ref) = rest[:-2], rest[-2:]
    total = parts[0][...]
    for part in parts[1:]:
        total = total + part[...]
    increment_ref[...] = total
    equal = jnp.sum(back_ref[...], axis=0, keepdims=True)
    departures_ref[...] = jnp.where(valid_ref[...] > 0.0, innovation_ref[...] - equal, 0.0)


def per_device(
    perturbation,
    control,
    filter_length,
    modes,
    obs_weights,
    innovation,
    obs_tile,
    obs_column,
    obs_count,
):
    members, levels, rows, cols = perturbation.shape
    kinds = control.shape[1]
    lines = members * kinds
    n_mem, n_lat, n_lon = (lax.axis_size(a) for a in ("mem", "lat", "lon"))
    mem, lat, lon = (lax.axis_index(a) for a in ("mem", "lat", "lon"))
    slots = innovation.shape[0]
    share = levels // n_mem
    all_cols = cols * n_lon

    rate = jnp.exp(-1.0 / filter_length)
    rest = 1.0 - rate
    log = jnp.log1p(-rest)
    beta = rate * jnp.expm1(2.0 * rows * log) / jnp.expm1(2.0 * log)
    table = jnp.tile(jnp.stack([log, rate, beta], axis=1), (members, 1))
    lons = jnp.stack([source(lon, s, n_lon) for s in range(n_lon)]).astype(jnp.int32)

    def ends(place):
        reach = (all_cols - place * cols - jnp.arange(cols)).astype(F32)
        return (rest * rest)[:, None] * -jnp.expm1(2.0 * log[:, None] * reach[None, :])

    matrix = pl.pallas_call(
        matrix_kernel,
        out_shape=jax.ShapeDtypeStruct((kinds, all_cols, 2 * cols), BF16),
        in_specs=[SMEM] + [VMEM] * 4,
        out_specs=VMEM,
        **params(8 * kinds * all_cols * cols, 4 * kinds * all_cols * cols, 5 * kinds * all_cols * cols),
    )(
        lons * cols,
        log[:, None],
        log[None],
        ends(lon),
        jnp.stack([ends(source(lon, s, n_lon)).T for s in range(n_lon)]),
    )

    whole = control.astype(F32)
    others = [send(whole, "lon", s) for s in range(1, n_lon)]
    others = jnp.stack(others) if others else jnp.zeros((1,) + whole.shape, F32)
    field, edge = pl.pallas_call(
        columns_kernel,
        out_shape=(
            jax.ShapeDtypeStruct((rows * (lines + 8), cols), F32),
            jax.ShapeDtypeStruct((2, lines, cols), F32),
        ),
        in_specs=[VMEM] * 4,
        out_specs=(VMEM, VMEM),
        scratch_shapes=[pltpu.VMEM((rows * lines, cols), F32)],
        **params(
            4 * lines * rows * cols * all_cols,
            4 * 2**20,
            4 * lines * rows * (2 * cols + all_cols) + 4 * kinds * all_cols * cols,
        ),
    )(control, others, matrix, table)

    obs_weights, obs_tile, obs_column, slot, _ = lax.optimization_barrier(
        (obs_weights, obs_tile, obs_column, jnp.arange(slots, dtype=jnp.int32), edge)
    )
    target = obs_tile[:, 0]
    fine_row = target // n_lon * (2 * rows) + obs_column // (2 * cols)
    fine_col = target % n_lon * (2 * cols) + obs_column % (2 * cols)
    weights = obs_weights.astype(F32).T
    places = jnp.stack([fine_row, fine_col]).astype(F32)
    packed = jnp.concatenate([weights, places, jnp.zeros((6, slots), F32)])

    edges = [edge] + [send(edge, "lat", s) for s in range(1, n_lat)]
    near = [packed[None]] + [send(packed[None], "lon", s) for s in range(1, n_lon)]
    edges = jnp.stack(edges)
    packed = [send(packed, "lat", s) for s in range(1, n_lat)]
    lats = jnp.stack([source(lat, s, n_lat) for s in range(n_lat)]).astype(jnp.int32)
    chunks = jnp.stack([toward(mem, r, n_mem) for r in range(n_mem)]).astype(jnp.int32)
    chunk_shape = jax.ShapeDtypeStruct((share * rows, cols), F32)
    sums = pl.pallas_call(
        functools.partial(sum_kernel, 1.0 / math.sqrt(members * n_mem - 1)),
        out_shape=(chunk_shape,) * n_mem,
        in_specs=[SMEM, SMEM] + [VMEM] * 5,
        out_specs=(VMEM,) * n_mem,
        scratch_shapes=[
            pltpu.VMEM((rows * lines, cols), F32),
            pltpu.VMEM((3 * lines, rows * cols), BF16),
            pltpu.VMEM((members * levels * (rows + 4), cols), F32),
            pltpu.VMEM((levels, kinds), F32),
        ],
        **params(
            6 * members * levels * lines * rows * cols,
            6 * 2**20,
            (7 * members + 4) * levels * rows * cols + 14 * lines * rows * cols,
        ),
    )(lats, chunks, table, edges, field, modes.T, perturbation)


    tiles = n_lat * n_lon
    origin = jnp.stack([lat * rows, lon * cols]).astype(jnp.int32)
    block_flops, block_size = 2 * levels * rows * cols * slots, 4 * (levels + 8) * slots
    equal, split = pl.pallas_call(
        functools.partial(near_kernel, levels, rows),
        out_shape=(
            jax.ShapeDtypeStruct((n_lon, slots), F32),
            jax.ShapeDtypeStruct((levels * rows, 2 * cols), BF16),
        ),
        in_specs=[SMEM] * 2 + [VMEM] * (n_mem + n_lon),
        out_specs=(VMEM, VMEM),
        **params(
            n_lon * block_flops, 2**20, 8 * levels * rows * cols + n_lon * block_size
        ),
    )(chunks, origin, *sums, *near)
    packs = []
    if n_lat > 1:
        packed = jnp.stack(lax.optimization_barrier((packed, equal))[0])
        packs = [packed] + [send(packed, "lon", s) for s in range(1, n_lon)]
    equal = pl.pallas_call(
        functools.partial(far_kernel, levels, rows),
        out_shape=jax.ShapeDtypeStruct((n_mem * tiles, slots), F32),
        in_specs=[SMEM] * 2 + [VMEM] * (2 + len(packs)),
        out_specs=VMEM,
        **params(
            (tiles - n_lon) * block_flops,
            4 * 2**20,
            4 * levels * rows * cols + tiles * block_size + n_mem * tiles * slots * 4,
        ),
    )(
        origin,
        jnp.concatenate(
            [lats[0] * n_lon + lons, (lats[None, 1:] * n_lon + lons[:, None]).reshape(-1)]
        ),
        split,
        equal,
        *packs,
    )

    held, leaving = [[chunk] for chunk in sums], equal
    if paired(n_mem):
        step = 1
        while step < n_mem:
            for r in reversed(range(step, n_mem, 2 * step)):
                part = functools.reduce(jnp.add, held[r])
                if 2 * step == n_mem:
                    leaving = lax.optimization_barrier((equal, part))[0]
                got = send(part, "mem", step)
                if r == 3:
                    got, _ = lax.optimization_barrier((got, equal))
                held[r ^ step].append(got)
            step *= 2
    else:
        for r in range(1, n_mem):
            held[0].append(send(sums[r], "mem", r))
    back = lax.all_to_all(leaving, ("mem", "lat", "lon"), 0, 0, tiled=True)
    increment, departures = pl.pallas_call(
        finish_kernel,
        out_shape=(chunk_shape, jax.ShapeDtypeStruct((1, slots), F32)),
        in_specs=[VMEM] * (3 + len(held[0])),
        out_specs=(VMEM, VMEM),
        **params(
            len(held[0]) * share * rows * cols,
            8 * len(held[0]) * share * rows * cols,
            8 * (len(held[0]) + 1) * share * rows * cols + 8 * n_mem * tiles * slots,
        ),
    )((slot < obs_count[0]).astype(F32)[None], innovation[None], back, *held[0])
    increment, departures = increment.reshape(share, rows, cols), departures[0]
    return (increment, departures)


def solution(mesh):
    placed = (
        P("mem", None, "lat", "lon"),
        P("mem", None, "lat", "lon"),
        P(),
        P(),
        P(("lat", "lon"), None),
        P(("lat", "lon")),
        P(("lat", "lon"), None),
        P(("lat", "lon")),
        P(("lat", "lon")),
    )
    return jax.shard_map(
        per_device,
        mesh=mesh,
        in_specs=placed,
        out_specs=(P("mem", "lat", "lon"), P(("lat", "lon"))),
        check_vma=False,
    )
```

```python
import functools
import math

import jax
import jax.numpy as jnp
from jax import lax
from jax.experimental import pallas as pl
from jax.experimental.pallas import tpu as pltpu
from jax.sharding import PartitionSpec as P

F32, BF16 = jnp.float32, jnp.bfloat16
VMEM = pl.BlockSpec(memory_space=pltpu.VMEM)
SMEM = pl.BlockSpec(memory_space=pltpu.SMEM)


def params(flops, moved, held):
    return dict(
        compiler_params=pltpu.CompilerParams(vmem_limit_bytes=held + 2 * 2**20),
        cost_estimate=pl.CostEstimate(flops=flops, bytes_accessed=moved, transcendentals=0),
    )


def paired(count):
    return count & (count - 1) == 0


def toward(place, step, count):
    return place ^ step if paired(count) else (place + step) % count


def source(place, step, count):
    return place ^ step if paired(count) else (place - step) % count


def send(block, axis, step):
    count = lax.axis_size(axis)
    return lax.ppermute(block, axis, [(i, toward(i, step, count)) for i in range(count)])


def collect(block, axis):
    count = lax.axis_size(axis)
    blocks = block[None]
    if not paired(count):
        return jnp.concatenate([blocks] + [send(blocks, axis, s) for s in range(1, count)])
    step = 1
    while step < count:
        blocks = jnp.concatenate([blocks, send(blocks, axis, step)])
        step *= 2
    return blocks


def halve(value):
    high = value.astype(BF16)
    return high, (value - high.astype(F32)).astype(BF16)


def matrix_kernel(starts_ref, log_ref, log_row_ref, to_ref, from_ref, matrix_ref):
    sources, cols, modes = from_ref.shape
    own = starts_ref[0]

    def put(s, k, value):
        high, low = halve(value)
        matrix_ref[k, s * cols : (s + 1) * cols, :] = jnp.concatenate([high, low], axis=1)

    across = lax.broadcasted_iota(jnp.int32, (cols, cols), 1)
    down = lax.broadcasted_iota(jnp.int32, (cols, cols), 0)
    distance = jnp.abs(across - down).astype(F32)
    for k in range(modes):
        end = jnp.where(across >= down, to_ref[k : k + 1, :], from_ref[0, :, k : k + 1])
        put(0, k, jnp.exp(distance * log_ref[k : k + 1, :1]) * end)
    for s in range(1, sources):
        there = starts_ref[s]
        between = jnp.maximum(own, there)
        before = there < own
        row = own + lax.broadcasted_iota(jnp.int32, (modes, cols), 1) - between
        row = jnp.exp(jnp.abs(row).astype(F32) * log_ref[...])
        row = row * jnp.where(before, to_ref[...], 1.0)
        column = there + lax.broadcasted_iota(jnp.int32, (cols, modes), 0) - between
        column = jnp.exp(jnp.abs(column).astype(F32) * log_row_ref[...])
        column = column * jnp.where(before, 1.0, from_ref[s])
        for k in range(modes):
            put(s, k, column[:, k : k + 1] * row[k : k + 1, :])


def columns_kernel(own_ref, other_ref, matrix_ref, table_ref, field_ref, edge_ref, first):
    members, modes, rows, cols = own_ref.shape
    sources = matrix_ref.shape[1] // cols
    lines = members * modes
    pitch = field_ref.shape[0] // rows
    for k in range(modes):
        pieces = [jnp.concatenate([own_ref[m, k] for m in range(members)])]
        for s in range(1, sources):
            pieces.append(
                jnp.concatenate([other_ref[s - 1, m, k] for m in range(members)]).astype(BF16)
            )
        both = jnp.dot(
            jnp.concatenate(pieces, axis=1), matrix_ref[k], preferred_element_type=F32
        )
        made = both[:, :cols] + both[:, cols:]
        for m in range(members):
            field_ref[pl.ds(m * modes + k, rows, stride=pitch), :] = made[m * rows : (m + 1) * rows]
    decay = jnp.broadcast_to(table_ref[:, 1:2], (lines, cols))
    state = jnp.zeros((lines, cols), F32)
    for x in range(rows):
        state = decay * state + field_ref[x * pitch : x * pitch + lines, :]
        first[x * lines : (x + 1) * lines, :] = state
    edge_ref[0] = state
    state = jnp.zeros((lines, cols), F32)
    for x in reversed(range(rows)):
        state = decay * state + first[x * lines : (x + 1) * lines, :]
    edge_ref[1] = state


def sum_kernel(
    scale, places_ref, chunks_ref, table_ref, edges_ref, field_ref, modes_ref, pert_ref, *rest
):
    chunks = len(rest) - 4
    outs, (first, second, pert, turned) = rest[:chunks], rest[chunks:]
    members, levels, rows, cols = pert_ref.shape
    lines, kinds = table_ref.shape[0], table_ref.shape[0] // members
    share = levels // chunks
    count = edges_ref.shape[0]
    pitch = pert.shape[0] // (members * levels)
    field_pitch = field_ref.shape[0] // rows

    for m in range(members):
        for z in range(levels):
            at = (m * levels + z) * pitch
            pert[at : at + rows, :] = pert_ref[m, z].astype(F32)

    log, decay, beta = (
        jnp.broadcast_to(table_ref[:, i : i + 1], (lines, cols)) for i in range(3)
    )

    def power(ahead):
        exponent = (rows * jnp.maximum(ahead, 0)).astype(F32)
        return jnp.where(ahead >= 0, jnp.exp(log * exponent), 0.0)

    own = places_ref[0]
    state = jnp.zeros((lines, cols), F32)
    after = jnp.zeros((lines, cols), F32)
    for s in range(count):
        there = places_ref[s]
        state = state + power(own - there - 1) * edges_ref[s, 0]
        before = jnp.zeros((lines, cols), F32)
        for t in range(count):
            before = before + power(there - places_ref[t] - 1) * edges_ref[t, 0]
        after = after + power(there - own - 1) * (edges_ref[s, 1] + beta * before)

    for x in range(rows):
        state = decay * state + field_ref[x * field_pitch : x * field_pitch + lines, :]
        first[x * lines : (x + 1) * lines, :] = state
    state = after
    for x in reversed(range(rows)):
        state = decay * state + first[x * lines : (x + 1) * lines, :]
        high, low = halve(state)
        second[:, x * cols : (x + 1) * cols] = jnp.concatenate([high, low, high])

    turned[...] = (modes_ref[...] * scale).T
    held = jnp.concatenate([turned[pl.ds(chunks_ref[r] * share, share), :] for r in range(chunks)])
    held = jnp.concatenate([held] * members, axis=1)
    member = lax.broadcasted_iota(jnp.int32, (levels, lines), 1) // kinds
    high, low = halve(
        jnp.concatenate([jnp.where(member == m, held, 0.0) for m in range(members)])
    )
    weights = jnp.concatenate([high, high, low], axis=1)

    for pair in range(0, rows, 2):
        profile = jnp.dot(
            weights,
            second[:, pair * cols : (pair + 2) * cols],
            preferred_element_type=F32,
        )
        for half in range(2):
            x = pair + half
            for r in range(chunks):
                total = None
                for m in range(members):
                    at = (m * levels + chunks_ref[r] * share) * pitch + x
                    line = m * levels + r * share
                    term = (
                        profile[line : line + share, half * cols : (half + 1) * cols]
                        * pert[pl.ds(at, share, stride=pitch), :]
                    )
                    total = term if total is None else total + term
                outs[r][pl.ds(x, share, stride=rows), :] = total


def observed(levels, rows, origin_ref, packed_ref, block, split):
    slots, cols = packed_ref.shape[2], split.shape[1] // 2

    def spread(fine, origin, length):
        near = jnp.floor(fine * 0.5)
        far = near - 1.0 + 2.0 * (fine - 2.0 * near)
        cell = (lax.broadcasted_iota(jnp.int32, (length, slots), 0) + origin).astype(F32)
        return jnp.where(cell == near, 0.75, 0.0) + jnp.where(cell == far, 0.25, 0.0)

    group = math.gcd(levels, 16)
    fine = packed_ref[block, levels : levels + 8, :]
    across = spread(fine[1:2], origin_ref[1], cols).astype(BF16)
    across = jnp.concatenate([across, across])
    down = spread(fine[0:1], origin_ref[0], rows)
    total = jnp.zeros((rows, slots), F32)
    for g in range(0, levels, group):
        seen = jnp.dot(
            split[g * rows : (g + group) * rows, :], across, preferred_element_type=F32
        )
        weights = packed_ref[block, g : g + group, :]
        for z in range(group):
            total = total + seen[z * rows : (z + 1) * rows] * weights[z : z + 1]
    return jnp.sum(total * down, axis=0, keepdims=True)


def near_kernel(levels, rows, chunks_ref, origin_ref, *rest):
    chunks = chunks_ref.shape[0]
    sums, packs, (out_ref, split) = rest[:chunks], rest[chunks:-2], rest[-2:]
    step = sums[0].shape[0]
    for r in range(chunks):
        high, low = halve(sums[r][...])
        at = pl.multiple_of(chunks_ref[r] * step, step)
        split[pl.ds(at, step), :] = jnp.concatenate([high, low], axis=1)
    for i, packed_ref in enumerate(packs):
        out_ref[i : i + 1, :] = observed(levels, rows, origin_ref, packed_ref, 0, split)


def far_kernel(levels, rows, origin_ref, spots_ref, split, near_ref, *rest):
    packs, out_ref = rest[:-1], rest[-1]
    tiles = spots_ref.shape[0]

    def put(place, row):
        for copy in range(out_ref.shape[0] // tiles):
            out_ref[pl.ds(copy * tiles + spots_ref[place], 1), :] = row

    before = near_ref.shape[0]
    for i in range(before):
        put(i, near_ref[i : i + 1, :])
    for packed_ref in packs:

        @pl.loop(0, packed_ref.shape[0], unroll=True)
        def _(block, packed_ref=packed_ref, before=before):
            put(before + block, observed(levels, rows, origin_ref, packed_ref, block, split))

        before += packed_ref.shape[0]


def finish_kernel(valid_ref, innovation_ref, back_ref, *rest):
    parts, (increment_ref, departures_ref) = rest[:-2], rest[-2:]
    total = parts[0][...]
    for part in parts[1:]:
        total = total + part[...]
    increment_ref[...] = total
    equal = jnp.sum(back_ref[...], axis=0, keepdims=True)
    departures_ref[...] = jnp.where(valid_ref[...] > 0.0, innovation_ref[...] - equal, 0.0)


def per_device(
    perturbation,
    control,
    filter_length,
    modes,
    obs_weights,
    innovation,
    obs_tile,
    obs_column,
    obs_count,
):
    members, levels, rows, cols = perturbation.shape
    kinds = control.shape[1]
    lines = members * kinds
    n_mem, n_lat, n_lon = (lax.axis_size(a) for a in ("mem", "lat", "lon"))
    mem, lat, lon = (lax.axis_index(a) for a in ("mem", "lat", "lon"))
    slots = innovation.shape[0]
    share = levels // n_mem
    all_cols = cols * n_lon

    rate = jnp.exp(-1.0 / filter_length)
    rest = 1.0 - rate
    log = jnp.log1p(-rest)
    beta = rate * jnp.expm1(2.0 * rows * log) / jnp.expm1(2.0 * log)
    table = jnp.tile(jnp.stack([log, rate, beta], axis=1), (members, 1))
    lons = jnp.stack([source(lon, s, n_lon) for s in range(n_lon)]).astype(jnp.int32)

    def ends(place):
        reach = (all_cols - place * cols - jnp.arange(cols)).astype(F32)
        return (rest * rest)[:, None] * -jnp.expm1(2.0 * log[:, None] * reach[None, :])

    matrix = pl.pallas_call(
        matrix_kernel,
        out_shape=jax.ShapeDtypeStruct((kinds, all_cols, 2 * cols), BF16),
        in_specs=[SMEM] + [VMEM] * 4,
        out_specs=VMEM,
        **params(8 * kinds * all_cols * cols, 4 * kinds * all_cols * cols, 5 * kinds * all_cols * cols),
    )(
        lons * cols,
        log[:, None],
        log[None],
        ends(lon),
        jnp.stack([ends(source(lon, s, n_lon)).T for s in range(n_lon)]),
    )

    whole = control.astype(F32)
    others = [send(whole, "lon", s) for s in range(1, n_lon)]
    others = jnp.stack(others) if others else jnp.zeros((1,) + whole.shape, F32)
    field, edge = pl.pallas_call(
        columns_kernel,
        out_shape=(
            jax.ShapeDtypeStruct((rows * (lines + 8), cols), F32),
            jax.ShapeDtypeStruct((2, lines, cols), F32),
        ),
        in_specs=[VMEM] * 4,
        out_specs=(VMEM, VMEM),
        scratch_shapes=[pltpu.VMEM((rows * lines, cols), F32)],
        **params(
            4 * lines * rows * cols * all_cols,
            4 * 2**20,
            4 * lines * rows * (2 * cols + all_cols) + 4 * kinds * all_cols * cols,
        ),
    )(control, others, matrix, table)

    obs_weights, obs_tile, obs_column, slot, _ = lax.optimization_barrier(
        (obs_weights, obs_tile, obs_column, jnp.arange(slots, dtype=jnp.int32), edge)
    )
    target = obs_tile[:, 0]
    fine_row = target // n_lon * (2 * rows) + obs_column // (2 * cols)
    fine_col = target % n_lon * (2 * cols) + obs_column % (2 * cols)
    weights = obs_weights.astype(F32).T
    places = jnp.stack([fine_row, fine_col]).astype(F32)
    packed = jnp.concatenate([weights, places, jnp.zeros((6, slots), F32)])

    edges = [edge] + [send(edge, "lat", s) for s in range(1, n_lat)]
    near = [packed[None]] + [send(packed[None], "lon", s) for s in range(1, n_lon)]
    edges = jnp.stack(edges)
    packed = [send(packed, "lat", s) for s in range(1, n_lat)]
    lats = jnp.stack([source(lat, s, n_lat) for s in range(n_lat)]).astype(jnp.int32)
    chunks = jnp.stack([toward(mem, r, n_mem) for r in range(n_mem)]).astype(jnp.int32)
    chunk_shape = jax.ShapeDtypeStruct((share * rows, cols), F32)
    sums = pl.pallas_call(
        functools.partial(sum_kernel, 1.0 / math.sqrt(members * n_mem - 1)),
        out_shape=(chunk_shape,) * n_mem,
        in_specs=[SMEM, SMEM] + [VMEM] * 5,
        out_specs=(VMEM,) * n_mem,
        scratch_shapes=[
            pltpu.VMEM((rows * lines, cols), F32),
            pltpu.VMEM((3 * lines, rows * cols), BF16),
            pltpu.VMEM((members * levels * (rows + 4), cols), F32),
            pltpu.VMEM((levels, kinds), F32),
        ],
        **params(
            6 * members * levels * lines * rows * cols,
            6 * 2**20,
            (7 * members + 4) * levels * rows * cols + 14 * lines * rows * cols,
        ),
    )(lats, chunks, table, edges, field, modes.T, perturbation)


    tiles = n_lat * n_lon
    origin = jnp.stack([lat * rows, lon * cols]).astype(jnp.int32)
    block_flops, block_size = 2 * levels * rows * cols * slots, 4 * (levels + 8) * slots
    equal, split = pl.pallas_call(
        functools.partial(near_kernel, levels, rows),
        out_shape=(
            jax.ShapeDtypeStruct((n_lon, slots), F32),
            jax.ShapeDtypeStruct((levels * rows, 2 * cols), BF16),
        ),
        in_specs=[SMEM] * 2 + [VMEM] * (n_mem + n_lon),
        out_specs=(VMEM, VMEM),
        **params(
            n_lon * block_flops, 2**20, 8 * levels * rows * cols + n_lon * block_size
        ),
    )(chunks, origin, *sums, *near)
    packs = []
    if n_lat > 1:
        packed = jnp.stack(lax.optimization_barrier((packed, equal))[0])
        packs = [packed] + [send(packed, "lon", s) for s in range(1, n_lon)]
    equal = pl.pallas_call(
        functools.partial(far_kernel, levels, rows),
        out_shape=jax.ShapeDtypeStruct((n_mem * tiles, slots), F32),
        in_specs=[SMEM] * 2 + [VMEM] * (2 + len(packs)),
        out_specs=VMEM,
        **params(
            (tiles - n_lon) * block_flops,
            4 * 2**20,
            4 * levels * rows * cols + tiles * block_size + n_mem * tiles * slots * 4,
        ),
    )(
        origin,
        jnp.concatenate(
            [lats[0] * n_lon + lons, (lats[None, 1:] * n_lon + lons[:, None]).reshape(-1)]
        ),
        split,
        equal,
        *packs,
    )

    held, leaving = [[chunk] for chunk in sums], equal
    if paired(n_mem):
        step = 1
        while step < n_mem:
            for r in reversed(range(step, n_mem, 2 * step)):
                part = functools.reduce(jnp.add, held[r])
                if 2 * step == n_mem:
                    leaving = lax.optimization_barrier((equal, part))[0]
                got = send(part, "mem", step)
                if r == 3:
                    got, _ = lax.optimization_barrier((got, equal))
                held[r ^ step].append(got)
            step *= 2
    else:
        for r in range(1, n_mem):
            held[0].append(send(sums[r], "mem", r))
    back = lax.all_to_all(leaving, ("mem", "lat", "lon"), 0, 0, tiled=True)
    increment, departures = pl.pallas_call(
        finish_kernel,
        out_shape=(chunk_shape, jax.ShapeDtypeStruct((1, slots), F32)),
        in_specs=[VMEM] * (3 + len(held[0])),
        out_specs=(VMEM, VMEM),
        **params(
            len(held[0]) * share * rows * cols,
            8 * len(held[0]) * share * rows * cols,
            8 * (len(held[0]) + 1) * share * rows * cols + 8 * n_mem * tiles * slots,
        ),
    )((slot < obs_count[0]).astype(F32)[None], innovation[None], back, *held[0])
    increment, departures = increment.reshape(share, rows, cols), departures[0]
    return (increment, departures)


def solution(mesh):
    placed = (
        P("mem", None, "lat", "lon"),
        P("mem", None, "lat", "lon"),
        P(),
        P(),
        P(("lat", "lon"), None),
        P(("lat", "lon")),
        P(("lat", "lon"), None),
        P(("lat", "lon")),
        P(("lat", "lon")),
    )
    return jax.shard_map(
        per_device,
        mesh=mesh,
        in_specs=placed,
        out_specs=(P("mem", "lat", "lon"), P(("lat", "lon"))),
        check_vma=False,
    )
```
